32 devices in a mesh: expert: 8 (over y, x, core), hidden: 4 (over z).
Axes of the slice: x: 2, y: 2, z: 4, core: 2. Of those that a mesh axis runs over, the one named last changes fastest.
Arguments:
- tokens: bfloat16 [16, 196, 1024], P('expert', None, 'hidden'), may hold values from -64 to 64
- slot_params: bfloat16 [1024, 8], P('hidden'), may hold values from -0.4 to 0.4
- weight_in: bfloat16 [8, 1024, 4096], P('expert', None, 'hidden'), may hold values from -0.1875 to 0.1875
- bias_in: bfloat16 [8, 4096], P('expert', 'hidden'), may hold values from -3 to 3
- weight_out: bfloat16 [8, 4096, 1024], P('expert', 'hidden'), may hold values from -0.09375 to 0.09375
- bias_out: bfloat16 [8, 1024], P('expert', 'hidden'), may hold values from -3 to 3
- cotangent: bfloat16 [16, 196, 1024], P('expert', None, 'hidden'), may hold values from -1.5 to 1.5
Outputs:
- mixed: bfloat16 [16, 196, 1024], P('expert', None, 'hidden')
- token_grad: bfloat16 [16, 196, 1024], P('expert', None, 'hidden')
- zloss: float32 [16, 196], P('expert')
The draws below stay inside these ranges and needn't reach their ends.
All inputs are finite; a program needn't handle non-finite values.
Results may differ from the reference program's by a relative error of at most 0.015.
Values may be sent and summed in bfloat16 or wider, within the bound.
No kernel may reach another device: no remote copies, remote signals or barrier semaphores. Data moves between devices by JAX's collectives and lax.ppermute only.
A program may use at most 64 MiB of HBM per device.

```python
import jax
import jax.numpy as jnp
from jax import lax

D = 1024
FF = 4096
TOK = 196
EXPERTS = 8
IMAGES = 16


def shared_params(key):
    base = jax.random.fold_in(key, 11)
    return 0.0625 * jnp.clip(jax.random.normal(base, (D, EXPERTS), jnp.float32), -6.0, 6.0)


def draw_slot_params(key, part):
    return shared_params(key).astype(jnp.bfloat16)


def draw_tokens(key, part):
    values = jnp.clip(jax.random.normal(jax.random.fold_in(key, 12), (IMAGES, TOK, D), jnp.float32), -6.0, 6.0)
    return values.astype(jnp.bfloat16)


def block_levels(own_key, dims, pieces, smallest, top_value):
    factor_of, own = 1.0, jax.random.fold_in(own_key, 6)
    for dim, parts in pieces:
        steps = jnp.exp(jax.random.uniform(jax.random.fold_in(own, dim), (parts,), jnp.float32, smallest / len(pieces), top_value / len(pieces)))
        factor_of = factor_of * jnp.repeat(steps, dims[dim] // parts).reshape([-1 if axis == dim else 1 for axis in range(len(dims))])
    return factor_of


def centred(rng, dims, width, reach, split=(), dtype=jnp.bfloat16):
    values = width * jax.random.normal(rng, dims, jnp.float32)
    if split:
        values = values * block_levels(rng, dims, split, -0.22, 0.18)
    return jnp.clip(values, -reach, reach).astype(dtype)


def setup_inputs(seed: int = 0) -> dict:
    seeds = jax.random.split(jax.random.key(seed), 8)
    return {
        "tokens": draw_tokens(jax.random.fold_in(seeds[7], 71), 0),
        "slot_params": draw_slot_params(jax.random.fold_in(seeds[7], 71), 0),
        "weight_in": centred(seeds[2], (EXPERTS, D, FF), D ** -0.5, 0.1875, ((0, 8), (2, 4))),
        "bias_in": centred(seeds[3], (EXPERTS, FF), 0.5, 3.0, ((0, 8), (1, 4))),
        "weight_out": centred(seeds[4], (EXPERTS, FF, D), FF ** -0.5, 0.09375, ((0, 8), (1, 4))),
        "bias_out": centred(seeds[5], (EXPERTS, D), 0.5, 3.0, ((0, 8), (1, 4))),
        "cotangent": centred(seeds[6], (IMAGES, TOK, D), 0.25, 1.5, ((0, 8), (2, 4))),
    }


loss_weight = 0.1


def gelu_parts(value):
    factor = 0.7978845608028654
    inner = factor * (value + 0.044715 * value * value * value)
    slope_tanh = jnp.tanh(inner)
    result = 0.5 * value * (1.0 + slope_tanh)
    slope = 0.5 * (1.0 + slope_tanh) + 0.5 * value * (1.0 - slope_tanh * slope_tanh) * factor * (1.0 + 3.0 * 0.044715 * value * value)
    return result, slope


def expert_step(inputs):
    slot_in, out_grad, w_first, b_first, w_second, b_second = inputs
    pre_act = jnp.dot(slot_in, w_first, preferred_element_type=jnp.float32) + b_first.astype(jnp.float32)
    activated, slope = gelu_parts(pre_act)
    act_low = activated.astype(jnp.bfloat16)
    slot_out = (jnp.dot(act_low, w_second, preferred_element_type=jnp.float32) + b_second.astype(jnp.float32)).astype(jnp.bfloat16)
    hidden_grad = jnp.dot(out_grad, w_second.T, preferred_element_type=jnp.float32)
    pre_grad = (hidden_grad * slope).astype(jnp.bfloat16)
    in_grad = jnp.dot(pre_grad, w_first.T, preferred_element_type=jnp.float32).astype(jnp.bfloat16)
    return slot_out, in_grad


def reference(tokens, slot_params, weight_in, bias_in, weight_out, bias_out, cotangent):
    tokens_wide = tokens.astype(jnp.float32)
    params_wide = slot_params.astype(jnp.float32)
    grad_wide = cotangent.astype(jnp.float32)
    logits = jnp.einsum("itd,ds->its", tokens_wide, params_wide)
    dispatch = jax.nn.softmax(logits, axis=1)
    combine = jax.nn.softmax(logits, axis=2)
    log_total = jax.nn.logsumexp(logits, axis=2)
    zloss = loss_weight * log_total * log_total
    dispatch_low = dispatch.astype(jnp.bfloat16)
    combine_low = combine.astype(jnp.bfloat16)
    slot_in = jnp.einsum("its,itd->isd", dispatch_low.astype(jnp.float32), tokens_wide).astype(jnp.bfloat16)
    out_grad = jnp.einsum("its,itd->isd", combine_low.astype(jnp.float32), grad_wide).astype(jnp.bfloat16)
    slot_out, in_grad = lax.map(expert_step, (jnp.transpose(slot_in, (1, 0, 2)), jnp.transpose(out_grad, (1, 0, 2)), weight_in, bias_in, weight_out, bias_out))
    slot_out = jnp.transpose(slot_out, (1, 0, 2)).astype(jnp.float32)
    in_grad = jnp.transpose(in_grad, (1, 0, 2)).astype(jnp.float32)
    mixed = jnp.einsum("its,isd->itd", combine_low.astype(jnp.float32), slot_out).astype(jnp.bfloat16)
    combine_grad = jnp.einsum("itd,isd->its", grad_wide, slot_out)
    dispatch_grad = jnp.einsum("itd,isd->its", tokens_wide, in_grad)
    from_combine = combine * (combine_grad - jnp.sum(combine * combine_grad, axis=2, keepdims=True)) + 2.0 * loss_weight * log_total[:, :, None] * combine
    from_dispatch = dispatch * (dispatch_grad - jnp.sum(dispatch * dispatch_grad, axis=1, keepdims=True))
    logit_grad = (from_combine + from_dispatch).astype(jnp.bfloat16).astype(jnp.float32)
    token_grad = jnp.einsum("its,ds->itd", logit_grad, params_wide) + jnp.einsum("its,isd->itd", dispatch_low.astype(jnp.float32), in_grad)
    return mixed, token_grad.astype(jnp.bfloat16), zloss
```

```python
import jax
import jax.numpy as jnp
import numpy as np
from jax import lax
from jax.experimental import pallas as pl
from jax.experimental.pallas import tpu as pltpu
from jax.sharding import PartitionSpec as P

loss_weight = 0.1
f32, bf16 = jnp.float32, jnp.bfloat16
VMEM = pl.BlockSpec(memory_space=pltpu.VMEM)
MIB = 1024 * 1024


def gelu_parts(value):
    factor = 0.7978845608028654
    inner = factor * (value + 0.044715 * value * value * value)
    slope_tanh = jnp.tanh(inner)
    result = 0.5 * value * (1.0 + slope_tanh)
    slope = 0.5 * (1.0 + slope_tanh) + 0.5 * value * (1.0 - slope_tanh * slope_tanh) * factor * (
        1.0 + 3.0 * 0.044715 * value * value
    )
    return (result, slope)


def dot(lhs, rhs, lhs_dim, rhs_dim):
    dims = (((lhs_dim,), (rhs_dim,)), ((), ()))
    return lax.dot_general(lhs, rhs, dims, preferred_element_type=f32)


def modulo(value, size):
    return value & (size - 1) if size & (size - 1) == 0 else lax.rem(value, size)


def iota(shape, dim):
    return lax.broadcasted_iota(jnp.int32, shape, dim)


def slot_masks(rows, tokens, images):
    place = modulo(iota((rows, tokens), 0), 2 * images)
    image = modulo(iota((rows, tokens), 1), images)
    return place == image, place == image + images


def spread(values, images):
    slots = values.shape[0]
    first = 2 * images * iota((2 * images * slots, slots), 1)
    row = iota((2 * images * slots, slots), 0)
    pick = jnp.where((row >= first) & (row < first + 2 * images), 1.0, 0.0).astype(bf16)
    return dot(pick, values, 1, 0)


def by_image(values, images, reduce, fill):
    image = modulo(iota(values.shape, 1), images)
    result = None
    for index in range(images):
        here = image == index
        part = reduce(jnp.where(here, values, fill), axis=1, keepdims=True)
        result = part if result is None else jnp.where(here, part, result)
    return jnp.broadcast_to(result, values.shape)


def logits_kernel(tokens_ref, keys_ref, part_ref, rows_ref):
    tokens, images, width = tokens_ref.shape
    rows = tokens_ref[...].reshape(tokens * images, width)
    rows_ref[...] = rows
    part_ref[...] = dot(keys_ref[...], rows, 1, 1)


def rows_kernel(tokens_ref, rows_ref):
    tokens, images, width = tokens_ref.shape
    rows_ref[...] = tokens_ref[...].reshape(tokens * images, width)


def tree_sum(refs):
    values = [ref[...].astype(f32) for ref in refs]
    while len(values) > 1:
        values = [values[k] + values[k + 1] for k in range(0, len(values), 2)]
    return values[0]


def dispatch_kernel(images, count, *refs):
    parts, (rows_ref, grads_ref, sent_ref, dispatch_ref, combine_ref, total_ref) = refs[:count], refs[count:]
    logits = tree_sum(parts)
    top = jnp.max(logits, axis=0, keepdims=True)
    powers = jnp.exp(logits - top)
    sums = jnp.sum(powers, axis=0, keepdims=True)
    combine = powers / sums
    total_ref[...] = top + jnp.log(sums)
    powers = jnp.exp(logits - by_image(logits, images, jnp.max, -jnp.inf))
    dispatch = powers / by_image(powers, images, jnp.sum, 0.0)
    combine_ref[...] = combine
    dispatch_ref[...] = dispatch
    slots, hidden, places, width = sent_ref.shape
    forward, backward = slot_masks(slots * places, logits.shape[1], images)
    left = jnp.where(forward, spread(dispatch.astype(bf16), images), 0.0).astype(bf16)
    right = jnp.where(backward, spread(combine.astype(bf16), images), 0.0).astype(bf16)
    sent = dot(left, rows_ref[...], 1, 0) + dot(right, grads_ref[...], 1, 0)
    sent = sent.astype(bf16).reshape(slots, places, width)
    for index in range(hidden):
        sent_ref[:, index] = sent


def expert_kernel(images, came_ref, win_ref, bin_ref, wout_ref, bout_ref, sent_ref):
    groups, hidden, places, width = came_ref.shape
    rows = groups * places
    came = jnp.concatenate([came_ref[:, index].reshape(rows, width) for index in range(hidden)], axis=1)
    pre = dot(came, win_ref[...], 1, 0) + bin_ref[...].astype(f32)
    hidden_grad = dot(came, wout_ref[...], 1, 1)
    activated, slope = gelu_parts(pre)
    out = dot(activated.astype(bf16), wout_ref[...], 1, 0) + bout_ref[...]
    pre_grad = (hidden_grad * pltpu.roll(slope, images, 0)).astype(bf16)
    back = dot(pre_grad, win_ref[...], 1, 1)
    forward = modulo(iota(out.shape, 0), places) < images
    sent = jnp.where(forward, out, back).astype(bf16)
    for index in range(hidden):
        sent_ref[:, index] = sent[:, index * width : (index + 1) * width].reshape(groups, places, width)


def gradient_kernel(images, came_ref, rows_ref, grads_ref, dispatch_ref, combine_ref, slots_ref, part_ref):
    slots, hidden, places, width = came_ref.shape
    came = came_ref[:, 0].astype(f32)
    for index in range(1, hidden):
        came = came + came_ref[:, index].astype(f32)
    came = came.reshape(slots * places, width).astype(bf16)
    slots_ref[...] = came
    tokens = rows_ref.shape[0]
    forward, backward = slot_masks(slots * places, tokens, images)
    combine_grad = jnp.where(forward, dot(came, grads_ref[...], 1, 1), 0.0)
    dispatch_grad = jnp.where(backward, dot(came, rows_ref[...], 1, 1), 0.0)
    combine_grad = jnp.sum(combine_grad.reshape(slots, places, tokens), axis=1)
    dispatch_grad = jnp.sum(dispatch_grad.reshape(slots, places, tokens), axis=1)
    combine, dispatch = combine_ref[...], dispatch_ref[...]
    part = combine * (combine_grad - jnp.sum(combine * combine_grad, axis=0, keepdims=True))
    part = part + dispatch * (dispatch_grad - by_image(dispatch * dispatch_grad, images, jnp.sum, 0.0))
    part_ref[...] = part.astype(bf16)


def mixed_kernel(images, combine_ref, slots_ref, out_ref):
    forward, _ = slot_masks(slots_ref.shape[0], combine_ref.shape[1], images)
    left = jnp.where(forward, spread(combine_ref[...].astype(bf16), images), 0.0).astype(bf16)
    out_ref[...] = dot(left, slots_ref[...], 0, 0).astype(bf16).reshape(out_ref.shape)


def token_kernel(images, count, *refs):
    parts, (dispatch_ref, combine_ref, total_ref, keys_ref, slots_ref, out_ref) = refs[:count], refs[count:]
    combine = combine_ref[...]
    logit_grad = tree_sum(parts) + 2.0 * loss_weight * total_ref[...] * combine
    _, backward = slot_masks(slots_ref.shape[0], combine.shape[1], images)
    left = jnp.where(backward, spread(dispatch_ref[...].astype(bf16), images), 0.0).astype(bf16)
    out = dot(logit_grad.astype(bf16), keys_ref[...], 0, 0) + dot(left, slots_ref[...], 0, 0)
    out_ref[...] = out.astype(bf16).reshape(out_ref.shape)


def call(kernel, outs, args, name, limit=8):
    return pl.pallas_call(
        kernel,
        out_shape=outs,
        in_specs=[VMEM] * len(args),
        out_specs=[VMEM] * len(outs),
        compiler_params=pltpu.CompilerParams(vmem_limit_bytes=limit * MIB),
        name=name,
    )(*args)


def exchange(value, axis):
    size = lax.axis_size(axis)
    return [value] + [
        lax.ppermute(value, axis, [(source, source ^ step) for source in range(size)])
        for step in range(1, size)
    ]


def per_device(tokens, slot_params, weight_in, bias_in, weight_out, bias_out, cotangent):
    images, count, width = tokens.shape
    groups, hidden = lax.axis_size("expert"), lax.axis_size("hidden")
    slots = slot_params.shape[1]
    wide = weight_in.shape[1]
    rows = images * count
    by_token = jnp.transpose(tokens, (1, 0, 2))
    grad_by_token = jnp.transpose(cotangent, (1, 0, 2))
    keys = jnp.transpose(slot_params)
    table = pltpu.VMEM((slots, rows), f32)
    sent_shape = pltpu.VMEM((groups, hidden, 2 * images, width), bf16)

    part, token_rows = call(
        logits_kernel, [table, pltpu.VMEM((rows, width), bf16)], (by_token, keys), "logits"
    )
    (grad_rows,) = call(rows_kernel, [pltpu.VMEM((rows, width), bf16)], (grad_by_token,), "rows")
    parts = exchange(part, "hidden")
    sent, dispatch, combine, total = call(
        lambda *refs: dispatch_kernel(images, hidden, *refs),
        [sent_shape, table, table, pltpu.VMEM((1, rows), f32)],
        (*parts, token_rows, grad_rows),
        "dispatch",
    )
    zloss = jnp.transpose((loss_weight * total * total).reshape(count, images))

    def to_all(value):
        value = value.reshape(groups * hidden, 2 * images, width)
        value = lax.all_to_all(value, ("expert", "hidden"), split_axis=0, concat_axis=0, tiled=True)
        return value.reshape(groups, hidden, 2 * images, width)

    own = lax.axis_index("hidden")
    here = lax.broadcasted_iota(jnp.int32, (hidden, width), 0) == own
    bias = jnp.where(here, bias_out.astype(f32), 0.0).reshape(1, wide)
    (sent,) = call(
        lambda *refs: expert_kernel(images, *refs),
        [sent_shape],
        (to_all(sent), weight_in[0], bias_in, weight_out[0], bias),
        "expert",
        24,
    )
    slot_rows, part = call(
        lambda *refs: gradient_kernel(images, *refs),
        [pltpu.VMEM((2 * images * slots, width), bf16), pltpu.VMEM((slots, rows), bf16)],
        (to_all(sent), token_rows, grad_rows, dispatch, combine),
        "gradient",
    )
    out_shape = jax.ShapeDtypeStruct((count, images, width), bf16)
    parts = exchange(part, "hidden")
    (mixed,) = call(
        lambda *refs: mixed_kernel(images, *refs), [out_shape], (combine, slot_rows), "mixed"
    )
    (token_grad,) = call(
        lambda *refs: token_kernel(images, hidden, *refs),
        [out_shape],
        (*parts, dispatch, combine, total, keys, slot_rows),
        "token_grad",
    )
    return (jnp.transpose(mixed, (1, 0, 2)), jnp.transpose(token_grad, (1, 0, 2)), zloss)


def solution(mesh):
    return jax.shard_map(
        per_device,
        mesh=mesh,
        in_specs=(
            P("expert", None, "hidden"),
            P("hidden", None),
            P("expert", None, "hidden"),
            P("expert", "hidden"),
            P("expert", "hidden", None),
            P("expert", "hidden"),
            P("expert", None, "hidden"),
        ),
        out_specs=(P("expert", None, "hidden"), P("expert", None, "hidden"), P("expert", None)),
        check_vma=False,
    )
```

```python
import jax
import jax.numpy as jnp
from jax import lax
from jax.experimental import pallas as pl
from jax.experimental.pallas import tpu as pltpu
from jax.sharding import PartitionSpec as P

loss_weight = 0.1
f32, bf16 = jnp.float32, jnp.bfloat16
VMEM = pl.BlockSpec(memory_space=pltpu.VMEM)
HBM = pl.BlockSpec(memory_space=pltpu.HBM)
MIB = 1024 * 1024


def gelu_parts(value):
    factor = 0.7978845608028654
    inner = factor * (value + 0.044715 * value * value * value)
    slope_tanh = jnp.tanh(inner)
    result = 0.5 * value * (1.0 + slope_tanh)
    slope = 0.5 * (1.0 + slope_tanh) + 0.5 * value * (1.0 - slope_tanh * slope_tanh) * factor * (
        1.0 + 3.0 * 0.044715 * value * value
    )
    return (result, slope)


def dot(lhs, rhs, lhs_dim, rhs_dim):
    dims = (((lhs_dim,), (rhs_dim,)), ((), ()))
    return lax.dot_general(lhs, rhs, dims, preferred_element_type=f32)


def modulo(value, size):
    return value & (size - 1) if size & (size - 1) == 0 else lax.rem(value, size)


def iota(shape, dim):
    return lax.broadcasted_iota(jnp.int32, shape, dim)


def slot_masks(rows, tokens, images):
    place = modulo(iota((rows, tokens), 0), 2 * images)
    image = modulo(iota((rows, tokens), 1), images)
    return place == image, place == image + images


def spread(values, images):
    slots = values.shape[0]
    first = 2 * images * iota((2 * images * slots, slots), 1)
    row = iota((2 * images * slots, slots), 0)
    pick = jnp.where((row >= first) & (row < first + 2 * images), 1.0, 0.0).astype(bf16)
    return dot(pick, values, 1, 0)


def by_image(values, images, reduce, fill):
    image = modulo(iota(values.shape, 1), images)
    result = None
    for index in range(images):
        here = image == index
        part = reduce(jnp.where(here, values, fill), axis=1, keepdims=True)
        result = part if result is None else jnp.where(here, part, result)
    return jnp.broadcast_to(result, values.shape)


def load(sources, targets, sems):
    copies = [pltpu.make_async_copy(*pair, sems.at[k]) for k, pair in enumerate(zip(sources, targets))]
    for copy in copies:
        copy.start()
    return copies


def logits_kernel(tokens_ref, keys_in_ref, part_ref, rows_ref, keys_ref, held_ref, sems):
    tokens, images, width = tokens_ref.shape
    for copy in load((tokens_ref, keys_in_ref), (held_ref, keys_ref), sems):
        copy.wait()
    rows = held_ref[...].reshape(tokens * images, width)
    rows_ref[...] = rows
    part_ref[...] = dot(keys_ref[...], rows, 1, 1)


def prepare_kernel(axis, after_ref, tokens_ref, win_in_ref, bin_in_ref, wout_in_ref, bout_in_ref,
                   rows_ref, win_ref, bin_ref, wout_ref, bout_ref, held_ref, held_bout_ref, sems):
    del after_ref
    tokens, images, width = tokens_ref.shape
    sources = (tokens_ref, bout_in_ref, bin_in_ref, win_in_ref, wout_in_ref)
    copies = load(sources, (held_ref, held_bout_ref, bin_ref, win_ref, wout_ref), sems)
    for copy in copies[:2]:
        copy.wait()
    rows_ref[...] = held_ref[...].reshape(tokens * images, width)
    own = lax.axis_index(axis)
    for index in range(bout_ref.shape[1] // width):
        bias = jnp.where(own == index, held_bout_ref[...].astype(f32), 0.0)
        bout_ref[:, index * width : (index + 1) * width] = bias
    for copy in copies[2:]:
        copy.wait()


def tree_sum(refs):
    values = [ref[...].astype(f32) for ref in refs]
    while len(values) > 1:
        values = [values[k] + values[k + 1] for k in range(0, len(values), 2)]
    return values[0]


def dispatch_kernel(images, count, *refs):
    parts, (rows_ref, grads_ref, sent_ref, dispatch_ref, combine_ref, total_ref) = refs[:count], refs[count:]
    logits = tree_sum(parts)
    top = jnp.max(logits, axis=0, keepdims=True)
    powers = jnp.exp(logits - top)
    sums = jnp.sum(powers, axis=0, keepdims=True)
    combine = powers / sums
    total_ref[...] = top + jnp.log(sums)
    powers = jnp.exp(logits - by_image(logits, images, jnp.max, -jnp.inf))
    dispatch = powers / by_image(powers, images, jnp.sum, 0.0)
    combine_ref[...] = combine
    dispatch_ref[...] = dispatch
    slots, hidden, places, width = sent_ref.shape
    forward, backward = slot_masks(slots * places, logits.shape[1], images)
    left = jnp.where(forward, spread(dispatch.astype(bf16), images), 0.0).astype(bf16)
    right = jnp.where(backward, spread(combine.astype(bf16), images), 0.0).astype(bf16)
    sent = dot(left, rows_ref[...], 1, 0) + dot(right, grads_ref[...], 1, 0)
    sent = sent.astype(bf16).reshape(slots, places, width)
    for index in range(hidden):
        sent_ref[:, index] = sent


def expert_kernel(images, came_ref, win_ref, bin_ref, wout_ref, bout_ref, sent_ref):
    groups, hidden, places, width = came_ref.shape
    rows = groups * places
    came = jnp.concatenate([came_ref[:, index].reshape(rows, width) for index in range(hidden)], axis=1)
    units = win_ref.shape[1]
    step = 256 if units % 256 == 0 else units
    out, back = bout_ref[...], 0.0
    for start in range(0, units, step):
        part = slice(start, start + step)
        pre = dot(came, win_ref[:, part], 1, 0) + bin_ref[:, part].astype(f32)
        hidden_grad = dot(came, wout_ref[part], 1, 1)
        activated, slope = gelu_parts(pre)
        out = out + dot(activated.astype(bf16), wout_ref[part], 1, 0)
        pre_grad = (hidden_grad * pltpu.roll(slope, images, 0)).astype(bf16)
        back = back + dot(pre_grad, win_ref[:, part], 1, 1)
    forward = modulo(iota(out.shape, 0), places) < images
    sent = jnp.where(forward, out, back).astype(bf16)
    for index in range(hidden):
        sent_ref[:, index] = sent[:, index * width : (index + 1) * width].reshape(groups, places, width)


def gradient_kernel(images, came_ref, rows_ref, grads_ref, dispatch_ref, combine_ref, slots_ref, part_ref):
    slots, hidden, places, width = came_ref.shape
    came = came_ref[:, 0].astype(f32)
    for index in range(1, hidden):
        came = came + came_ref[:, index].astype(f32)
    came = came.reshape(slots * places, width).astype(bf16)
    slots_ref[...] = came
    tokens = rows_ref.shape[0]
    forward, backward = slot_masks(slots * places, tokens, images)
    combine_grad = jnp.where(forward, dot(came, grads_ref[...], 1, 1), 0.0)
    dispatch_grad = jnp.where(backward, dot(came, rows_ref[...], 1, 1), 0.0)
    combine_grad = jnp.sum(combine_grad.reshape(slots, places, tokens), axis=1)
    dispatch_grad = jnp.sum(dispatch_grad.reshape(slots, places, tokens), axis=1)
    combine, dispatch = combine_ref[...], dispatch_ref[...]
    part = combine * (combine_grad - jnp.sum(combine * combine_grad, axis=0, keepdims=True))
    part = part + dispatch * (dispatch_grad - by_image(dispatch * dispatch_grad, images, jnp.sum, 0.0))
    part_ref[...] = part.astype(bf16)


def mixed_kernel(images, dispatch_ref, combine_ref, slots_ref, out_ref, direct_ref):
    forward, backward = slot_masks(slots_ref.shape[0], combine_ref.shape[1], images)
    left = jnp.where(forward, spread(combine_ref[...].astype(bf16), images), 0.0).astype(bf16)
    out_ref[...] = dot(left, slots_ref[...], 0, 0).astype(bf16).reshape(out_ref.shape)
    left = jnp.where(backward, spread(dispatch_ref[...].astype(bf16), images), 0.0).astype(bf16)
    direct_ref[...] = dot(left, slots_ref[...], 0, 0)


def token_kernel(count, *refs):
    parts, (combine_ref, total_ref, keys_ref, direct_ref, out_ref) = refs[:count], refs[count:]
    logit_grad = tree_sum(parts) + 2.0 * loss_weight * total_ref[...] * combine_ref[...]
    out = dot(logit_grad.astype(bf16), keys_ref[...], 0, 0) + direct_ref[...]
    out_ref[...] = out.astype(bf16).reshape(out_ref.shape)


def stay(value):
    return pltpu.with_memory_space_constraint(value, pltpu.HBM)


def call(kernel, outs, args, name, limit=8, place=VMEM, scratch=()):
    return pl.pallas_call(
        kernel,
        out_shape=outs,
        in_specs=[place] * len(args),
        out_specs=[VMEM] * len(outs),
        scratch_shapes=scratch,
        compiler_params=pltpu.CompilerParams(vmem_limit_bytes=limit * MIB),
        name=name,
    )(*args)


def exchange(value, axis):
    size = lax.axis_size(axis)
    return [value] + [
        lax.ppermute(value, axis, [(source, source ^ step) for source in range(size)])
        for step in range(1, size)
    ]


def prepare(after, cotangent, weight_in, bias_in, weight_out, bias_out, row_shape, held_shape):
    wide = weight_in.shape[0]
    shapes = [pltpu.VMEM(value.shape, bf16) for value in (weight_in, bias_in, weight_out)]
    specs = [VMEM if value is after else HBM for value in (after, cotangent, weight_in, bias_in, weight_out, bias_out)]
    return pl.pallas_call(
        lambda *refs: prepare_kernel("hidden", *refs),
        out_shape=[row_shape, *shapes, pltpu.VMEM((1, wide), f32)],
        in_specs=specs,
        out_specs=[VMEM] * 5,
        scratch_shapes=[held_shape, pltpu.VMEM(bias_out.shape, bf16), pltpu.SemaphoreType.DMA((5,))],
        compiler_params=pltpu.CompilerParams(vmem_limit_bytes=16 * MIB),
        name="prepare",
    )(after, *map(stay, (cotangent, weight_in, bias_in, weight_out, bias_out)))


def per_device(tokens, slot_params, weight_in, bias_in, weight_out, bias_out, cotangent):
    images, count, width = tokens.shape
    groups, hidden = lax.axis_size("expert"), lax.axis_size("hidden")
    slots = slot_params.shape[1]
    rows = images * count
    by_token = jnp.transpose(tokens, (1, 0, 2))
    grad_by_token = jnp.transpose(cotangent, (1, 0, 2))
    table = pltpu.VMEM((slots, rows), f32)
    row_shape = pltpu.VMEM((rows, width), bf16)
    held_shape = pltpu.VMEM(by_token.shape, bf16)
    sent_shape = pltpu.VMEM((groups, hidden, 2 * images, width), bf16)

    part, token_rows, keys = call(
        logits_kernel,
        [table, row_shape, pltpu.VMEM((slots, width), bf16)],
        (stay(by_token), stay(jnp.transpose(slot_params))),
        "logits",
        place=HBM,
        scratch=[held_shape, pltpu.SemaphoreType.DMA((2,))],
    )
    grad_rows, win, bin_, wout, bout = prepare(
        part, grad_by_token, weight_in[0], bias_in, weight_out[0], bias_out, row_shape, held_shape
    )
    parts = exchange(part, "hidden")
    sent, dispatch, combine, total = call(
        lambda *refs: dispatch_kernel(images, hidden, *refs),
        [sent_shape, table, table, pltpu.VMEM((1, rows), f32)],
        (*parts, token_rows, grad_rows),
        "dispatch",
    )
    zloss = jnp.transpose((loss_weight * total * total).reshape(count, images))

    def to_all(value):
        value = value.reshape(groups * hidden, 2 * images, width)
        value = lax.all_to_all(value, ("expert", "hidden"), split_axis=0, concat_axis=0, tiled=True)
        return value.reshape(groups, hidden, 2 * images, width)

    (sent,) = call(
        lambda *refs: expert_kernel(images, *refs),
        [sent_shape],
        (to_all(sent), win, bin_, wout, bout),
        "expert",
        24,
    )
    slot_rows, part = call(
        lambda *refs: gradient_kernel(images, *refs),
        [pltpu.VMEM((2 * images * slots, width), bf16), pltpu.VMEM((slots, rows), bf16)],
        (to_all(sent), token_rows, grad_rows, dispatch, combine),
        "gradient",
    )
    out_shape = jax.ShapeDtypeStruct((count, images, width), bf16)
    parts = exchange(part, "hidden")
    mixed, direct = call(
        lambda *refs: mixed_kernel(images, *refs),
        [out_shape, pltpu.VMEM((rows, width), f32)],
        (dispatch, combine, slot_rows),
        "mixed",
    )
    (token_grad,) = call(
        lambda *refs: token_kernel(hidden, *refs),
        [out_shape],
        (*parts, combine, total, keys, direct),
        "token_grad",
    )
    return (jnp.transpose(mixed, (1, 0, 2)), jnp.transpose(token_grad, (1, 0, 2)), zloss)


def solution(mesh):
    return jax.shard_map(
        per_device,
        mesh=mesh,
        in_specs=(
            P("expert", None, "hidden"),
            P("hidden", None),
            P("expert", None, "hidden"),
            P("expert", "hidden"),
            P("expert", "hidden", None),
            P("expert", "hidden"),
            P("expert", None, "hidden"),
        ),
        out_specs=(P("expert", None, "hidden"), P("expert", None, "hidden"), P("expert", None)),
        check_vma=False,
    )
```

```python
import jax
import jax.numpy as jnp
from jax import lax
from jax.experimental import pallas as pl
from jax.experimental.pallas import tpu as pltpu
from jax.sharding import PartitionSpec as P

loss_weight = 0.1
f32, bf16 = jnp.float32, jnp.bfloat16
VMEM = pl.BlockSpec(memory_space=pltpu.VMEM)
HBM = pl.BlockSpec(memory_space=pltpu.HBM)
MIB = 1024 * 1024


def gelu_parts(value):
    factor = 0.7978845608028654
    inner = factor * (value + 0.044715 * value * value * value)
    slope_tanh = jnp.tanh(inner)
    result = 0.5 * value * (1.0 + slope_tanh)
    slope = 0.5 * (1.0 + slope_tanh) + 0.5 * value * (1.0 - slope_tanh * slope_tanh) * factor * (
        1.0 + 3.0 * 0.044715 * value * value
    )
    return (result, slope)


def dot(lhs, rhs, lhs_dim, rhs_dim):
    dims = (((lhs_dim,), (rhs_dim,)), ((), ()))
    return lax.dot_general(lhs, rhs, dims, preferred_element_type=f32)


def modulo(value, size):
    return value & (size - 1) if size & (size - 1) == 0 else lax.rem(value, size)


def iota(shape, dim):
    return lax.broadcasted_iota(jnp.int32, shape, dim)


def slot_masks(rows, tokens, images):
    place = modulo(iota((rows, tokens), 0), 2 * images)
    image = modulo(iota((rows, tokens), 1), images)
    return place == image, place == image + images


def spread(values, images):
    slots = values.shape[0]
    first = 2 * images * iota((2 * images * slots, slots), 1)
    row = iota((2 * images * slots, slots), 0)
    pick = jnp.where((row >= first) & (row < first + 2 * images), 1.0, 0.0).astype(bf16)
    return dot(pick, values, 1, 0)


def by_image(values, images, reduce, fill):
    image = modulo(iota(values.shape, 1), images)
    result = None
    for index in range(images):
        here = image == index
        part = reduce(jnp.where(here, values, fill), axis=1, keepdims=True)
        result = part if result is None else jnp.where(here, part, result)
    return jnp.broadcast_to(result, values.shape)


def load(sources, targets, sems):
    copies = [pltpu.make_async_copy(*pair, sems.at[k]) for k, pair in enumerate(zip(sources, targets))]
    for copy in copies:
        copy.start()
    return copies


def logits_kernel(tokens_ref, keys_in_ref, part_ref, rows_ref, keys_ref, held_ref, sems):
    tokens, images, width = tokens_ref.shape
    for copy in load((tokens_ref, keys_in_ref), (held_ref, keys_ref), sems):
        copy.wait()
    rows = held_ref[...].reshape(tokens * images, width)
    rows_ref[...] = rows
    part_ref[...] = dot(keys_ref[...], rows, 1, 1)


def prepare_kernel(axis, after_ref, tokens_ref, bout_in_ref, bin_in_ref, win_in_ref, wout_in_ref,
                   rows_ref, bout_ref, bin_ref, win_ref, wout_ref, held_ref, held_bout_ref, sems):
    del after_ref
    tokens, images, width = tokens_ref.shape
    sources = (tokens_ref, bout_in_ref, bin_in_ref, win_in_ref, wout_in_ref)
    copies = load(sources, (held_ref, held_bout_ref, bin_ref, win_ref, wout_ref), sems)
    for copy in copies[:2]:
        copy.wait()
    rows_ref[...] = held_ref[...].reshape(tokens * images, width)
    own = lax.axis_index(axis)
    for index in range(bout_ref.shape[1] // width):
        bias = jnp.where(own == index, held_bout_ref[...].astype(f32), 0.0)
        bout_ref[:, index * width : (index + 1) * width] = bias
    for copy in copies[2:]:
        copy.wait()


def steps(size):
    return [1] + list(range(size - 1, 1, -1))


def tree_sum(refs):
    order = [0] + steps(len(refs))
    values = [refs[order.index(step)][...].astype(f32) for step in range(len(refs))]
    while len(values) > 1:
        values = [values[k] + values[k + 1] for k in range(0, len(values), 2)]
    return values[0]


def dispatch_kernel(images, count, *refs):
    parts, (rows_ref, grads_ref, sent_ref, dispatch_ref, combine_ref, total_ref) = refs[:count], refs[count:]
    logits = tree_sum(parts)
    top = jnp.max(logits, axis=0, keepdims=True)
    powers = jnp.exp(logits - top)
    sums = jnp.sum(powers, axis=0, keepdims=True)
    combine = powers / sums
    total_ref[...] = top + jnp.log(sums)
    powers = jnp.exp(logits - by_image(logits, images, jnp.max, -jnp.inf))
    dispatch = powers / by_image(powers, images, jnp.sum, 0.0)
    combine_ref[...] = combine
    dispatch_ref[...] = dispatch
    slots, hidden, places, width = sent_ref.shape
    forward, backward = slot_masks(slots * places, logits.shape[1], images)
    left = jnp.where(forward, spread(dispatch.astype(bf16), images), 0.0).astype(bf16)
    right = jnp.where(backward, spread(combine.astype(bf16), images), 0.0).astype(bf16)
    sent = dot(left, rows_ref[...], 1, 0) + dot(right, grads_ref[...], 1, 0)
    sent = sent.astype(bf16).reshape(slots, places, width)
    for index in range(hidden):
        sent_ref[:, index] = sent


def expert_kernel(images, came_ref, win_ref, bin_ref, wout_ref, bout_ref, sent_ref):
    groups, hidden, places, width = came_ref.shape
    rows = groups * places
    came = jnp.concatenate([came_ref[:, index].reshape(rows, width) for index in range(hidden)], axis=1)
    pre = dot(came, win_ref[...], 1, 0) + bin_ref[...].astype(f32)
    hidden_grad = dot(came, wout_ref[...], 1, 1)
    activated, slope = gelu_parts(pre)
    out = dot(activated.astype(bf16), wout_ref[...], 1, 0) + bout_ref[...]
    pre_grad = (hidden_grad * pltpu.roll(slope, images, 0)).astype(bf16)
    back = dot(pre_grad, win_ref[...], 1, 1)
    forward = modulo(iota(out.shape, 0), places) < images
    sent = jnp.where(forward, out, back).astype(bf16)
    for index in range(hidden):
        sent_ref[:, index] = sent[:, index * width : (index + 1) * width].reshape(groups, places, width)


def gradient_kernel(images, came_ref, rows_ref, grads_ref, dispatch_ref, combine_ref, slots_ref, part_ref):
    slots, hidden, places, width = came_ref.shape
    came = came_ref[:, 0].astype(f32)
    for index in range(1, hidden):
        came = came + came_ref[:, index].astype(f32)
    came = came.reshape(slots * places, width).astype(bf16)
    slots_ref[...] = came
    tokens = rows_ref.shape[0]
    forward, backward = slot_masks(slots * places, tokens, images)
    combine_grad = jnp.where(forward, dot(came, grads_ref[...], 1, 1), 0.0)
    dispatch_grad = jnp.where(backward, dot(came, rows_ref[...], 1, 1), 0.0)
    combine_grad = jnp.sum(combine_grad.reshape(slots, places, tokens), axis=1)
    dispatch_grad = jnp.sum(dispatch_grad.reshape(slots, places, tokens), axis=1)
    combine, dispatch = combine_ref[...], dispatch_ref[...]
    part = combine * (combine_grad - jnp.sum(combine * combine_grad, axis=0, keepdims=True))
    part = part + dispatch * (dispatch_grad - by_image(dispatch * dispatch_grad, images, jnp.sum, 0.0))
    part_ref[...] = part.astype(bf16)


def mixed_kernel(images, dispatch_ref, combine_ref, total_ref, slots_ref, mixed_ref, direct_ref, loss_ref):
    forward, backward = slot_masks(slots_ref.shape[0], combine_ref.shape[1], images)
    left = jnp.where(forward, spread(combine_ref[...].astype(bf16), images), 0.0).astype(bf16)
    mixed_ref[...] = dot(left, slots_ref[...], 0, 0).astype(bf16).reshape(mixed_ref.shape)
    left = jnp.where(backward, spread(dispatch_ref[...].astype(bf16), images), 0.0).astype(bf16)
    direct_ref[...] = dot(left, slots_ref[...], 0, 0)
    total = jnp.broadcast_to(total_ref[...], (8, total_ref.shape[1]))
    tokens = loss_ref.shape[1]
    row, token = iota((images * tokens, tokens), 0), iota((images * tokens, tokens), 1)
    for index in range(images):
        pick = jnp.where(row == images * token + index, 1.0, 0.0)
        own = lax.dot_general(
            total, pick, (((1,), (0,)), ((), ())), precision=lax.Precision.HIGHEST, preferred_element_type=f32
        )[:1]
        loss_ref[index : index + 1] = loss_weight * own * own


def token_kernel(count, *refs):
    parts, refs = refs[:count], refs[count:]
    (combine_ref, total_ref, keys_ref, direct_ref, mixed_ref, loss_ref) = refs[:6]
    (out_ref, mixed_out_ref, loss_out_ref, held_ref, sems) = refs[6:]
    copies = load((mixed_ref, loss_ref), (mixed_out_ref, loss_out_ref), sems)
    logit_grad = tree_sum(parts) + 2.0 * loss_weight * total_ref[...] * combine_ref[...]
    out = dot(logit_grad.astype(bf16), keys_ref[...], 0, 0) + direct_ref[...]
    held_ref[...] = out.astype(bf16).reshape(held_ref.shape)
    last = pltpu.make_async_copy(held_ref, out_ref, sems.at[2])
    last.start()
    for copy in (*copies, last):
        copy.wait()


def call(kernel, outs, args, name, limit=8, far=(), far_outs=False, scratch=(), cost=None):
    return pl.pallas_call(
        kernel,
        out_shape=outs,
        in_specs=[VMEM] * len(args) + [HBM] * len(far),
        out_specs=[HBM if far_outs else VMEM] * len(outs),
        scratch_shapes=scratch,
        compiler_params=pltpu.CompilerParams(vmem_limit_bytes=limit * MIB),
        cost_estimate=cost,
        name=name,
    )(*args, *(pltpu.with_memory_space_constraint(value, pltpu.HBM) for value in far))


def exchange(value, axis):
    size = lax.axis_size(axis)
    return [value] + [
        lax.ppermute(value, axis, [(source, source ^ step) for source in range(size)]) for step in steps(size)
    ]


def per_device(tokens, slot_params, weight_in, bias_in, weight_out, bias_out, cotangent):
    images, count, width = tokens.shape
    groups, hidden = lax.axis_size("expert"), lax.axis_size("hidden")
    slots = slot_params.shape[1]
    wide = weight_in.shape[1]
    rows = images * count
    weight_in, weight_out = weight_in[0], weight_out[0]
    by_token = jnp.transpose(tokens, (1, 0, 2))
    grad_by_token = jnp.transpose(cotangent, (1, 0, 2))
    table = pltpu.VMEM((slots, rows), f32)
    row_shape = pltpu.VMEM((rows, width), bf16)
    held_shape = pltpu.VMEM(by_token.shape, bf16)
    sent_shape = pltpu.VMEM((groups, hidden, 2 * images, width), bf16)

    part, token_rows, keys = call(
        logits_kernel,
        [table, row_shape, pltpu.VMEM((slots, width), bf16)],
        (),
        "logits",
        far=(by_token, jnp.transpose(slot_params)),
        scratch=[held_shape, pltpu.SemaphoreType.DMA((2,))],
    )
    grad_rows, bias_out, bias_in, weight_in, weight_out = call(
        lambda *refs: prepare_kernel("hidden", *refs),
        [row_shape, pltpu.VMEM((1, wide), f32), *[pltpu.VMEM(v.shape, bf16) for v in (bias_in, weight_in, weight_out)]],
        (part,),
        "prepare",
        far=(grad_by_token, bias_out, bias_in, weight_in, weight_out),
        scratch=[held_shape, pltpu.VMEM(bias_out.shape, bf16), pltpu.SemaphoreType.DMA((5,))],
    )
    parts = exchange(part, "hidden")
    sent, dispatch, combine, total = call(
        lambda *refs: dispatch_kernel(images, hidden, *refs),
        [sent_shape, table, table, pltpu.VMEM((1, rows), f32)],
        (*parts, token_rows, grad_rows),
        "dispatch",
    )

    def to_all(value):
        value = value.reshape(groups * hidden, 2 * images, width)
        value = lax.all_to_all(value, ("expert", "hidden"), split_axis=0, concat_axis=0, tiled=True)
        return value.reshape(groups, hidden, 2 * images, width)

    (sent,) = call(
        lambda *refs: expert_kernel(images, *refs),
        [sent_shape],
        (to_all(sent), weight_in, bias_in, weight_out, bias_out),
        "expert",
        24,
    )
    slot_rows, part = call(
        lambda *refs: gradient_kernel(images, *refs),
        [pltpu.VMEM((2 * images * slots, width), bf16), pltpu.VMEM((slots, rows), bf16)],
        (to_all(sent), token_rows, grad_rows, dispatch, combine),
        "gradient",
    )
    parts = exchange(part, "hidden")
    mixed, direct, zloss = call(
        lambda *refs: mixed_kernel(images, *refs),
        [held_shape, pltpu.VMEM((rows, width), f32), pltpu.VMEM((images, count), f32)],
        (dispatch, combine, total, slot_rows),
        "mixed",
    )
    out_shape = jax.ShapeDtypeStruct(by_token.shape, bf16)
    token_grad, mixed, zloss = call(
        lambda *refs: token_kernel(hidden, *refs),
        [out_shape, out_shape, jax.ShapeDtypeStruct((images, count), f32)],
        (*parts, combine, total, keys, direct, mixed, zloss),
        "token_grad",
        far_outs=True,
        scratch=[held_shape, pltpu.SemaphoreType.DMA((3,))],
    )
    return (jnp.transpose(mixed, (1, 0, 2)), jnp.transpose(token_grad, (1, 0, 2)), zloss)


def solution(mesh):
    return jax.shard_map(
        per_device,
        mesh=mesh,
        in_specs=(
            P("expert", None, "hidden"),
            P("hidden", None),
            P("expert", None, "hidden"),
            P("expert", "hidden"),
            P("expert", "hidden", None),
            P("expert", "hidden"),
            P("expert", None, "hidden"),
        ),
        out_specs=(P("expert", None, "hidden"), P("expert", None, "hidden"), P("expert", None)),
        check_vma=False,
    )
```

```python
import jax
import jax.numpy as jnp
from jax import lax
from jax.experimental import pallas as pl
from jax.experimental.pallas import tpu as pltpu
from jax.sharding import PartitionSpec as P

loss_weight = 0.1
f32, bf16 = jnp.float32, jnp.bfloat16
VMEM = pl.BlockSpec(memory_space=pltpu.VMEM)
HBM = pl.BlockSpec(memory_space=pltpu.HBM)
MIB = 1024 * 1024


def gelu_parts(value):
    factor = 0.7978845608028654
    inner = factor * (value + 0.044715 * value * value * value)
    slope_tanh = jnp.tanh(inner)
    result = 0.5 * value * (1.0 + slope_tanh)
    slope = 0.5 * (1.0 + slope_tanh) + 0.5 * value * (1.0 - slope_tanh * slope_tanh) * factor * (
        1.0 + 3.0 * 0.044715 * value * value
    )
    return (result, slope)


def dot(lhs, rhs, lhs_dim, rhs_dim):
    dims = (((lhs_dim,), (rhs_dim,)), ((), ()))
    return lax.dot_general(lhs, rhs, dims, preferred_element_type=f32)


def modulo(value, size):
    return value & (size - 1) if size & (size - 1) == 0 else lax.rem(value, size)


def iota(shape, dim):
    return lax.broadcasted_iota(jnp.int32, shape, dim)


def same_image(rows, tokens, images):
    return modulo(iota((rows, tokens), 0), images) == modulo(iota((rows, tokens), 1), images)


def spread(values, images):
    slots, tokens = values.shape
    first = images * iota((images * slots, slots), 1)
    row = iota((images * slots, slots), 0)
    pick = jnp.where((row >= first) & (row < first + images), 1.0, 0.0).astype(bf16)
    wide = dot(pick, values.astype(bf16), 1, 0)
    return jnp.where(same_image(images * slots, tokens, images), wide, 0.0).astype(bf16)


def gather(values, images):
    rows, tokens = values.shape
    values = jnp.where(same_image(rows, tokens, images), values, 0.0)
    return jnp.sum(values.reshape(rows // images, images, tokens), axis=1)


def by_image(values, images, reduce, fill):
    image = modulo(iota(values.shape, 1), images)
    result = None
    for index in range(images):
        here = image == index
        part = reduce(jnp.where(here, values, fill), axis=1, keepdims=True)
        result = part if result is None else jnp.where(here, part, result)
    return jnp.broadcast_to(result, values.shape)


def load(sources, targets, sems):
    copies = [pltpu.make_async_copy(*pair, sems.at[k]) for k, pair in enumerate(zip(sources, targets))]
    for copy in copies:
        copy.start()
    return copies


def logits_kernel(tokens_ref, keys_in_ref, part_ref, rows_ref, keys_ref, held_ref, sems):
    tokens, images, width = tokens_ref.shape
    for copy in load((tokens_ref, keys_in_ref), (held_ref, keys_ref), sems):
        copy.wait()
    rows = held_ref[...].reshape(tokens * images, width)
    rows_ref[...] = rows
    part_ref[...] = dot(keys_ref[...], rows, 1, 1)


def prepare_kernel(axis, after_ref, tokens_ref, bout_in_ref, bin_in_ref, win_in_ref, wout_in_ref,
                   rows_ref, bout_ref, bin_ref, win_ref, wout_ref, held_ref, held_bout_ref, sems):
    del after_ref
    tokens, images, width = tokens_ref.shape
    sources = (tokens_ref, bout_in_ref, bin_in_ref, win_in_ref, wout_in_ref)
    copies = load(sources, (held_ref, held_bout_ref, bin_ref, win_ref, wout_ref), sems)
    for copy in copies[:2]:
        copy.wait()
    rows_ref[...] = held_ref[...].reshape(tokens * images, width)
    own = lax.axis_index(axis)
    for index in range(bout_ref.shape[1] // width):
        bias = jnp.where(own == index, held_bout_ref[...].astype(f32), 0.0)
        bout_ref[:, index * width : (index + 1) * width] = bias
    for copy in copies[2:]:
        copy.wait()


def steps(size, first):
    return [1] + list(range(size - 1, 1, -1)) if first else list(range(1, size))


def tree_sum(refs, first):
    order = [0] + steps(len(refs), first)
    values = [refs[order.index(step)][...].astype(f32) for step in range(len(refs))]
    while len(values) > 1:
        values = [values[k] + values[k + 1] for k in range(0, len(values), 2)]
    return values[0]


def dispatch_kernel(images, count, *refs):
    parts, (rows_ref, grads_ref, sent_ref, dispatch_ref, combine_ref, total_ref) = refs[:count], refs[count:]
    logits = tree_sum(parts, True)
    top = jnp.max(logits, axis=0, keepdims=True)
    powers = jnp.exp(logits - top)
    sums = jnp.sum(powers, axis=0, keepdims=True)
    combine = powers / sums
    total_ref[...] = top + jnp.log(sums)
    powers = jnp.exp(logits - by_image(logits, images, jnp.max, -jnp.inf))
    dispatch = powers / by_image(powers, images, jnp.sum, 0.0)
    combine_ref[...] = combine
    dispatch_ref[...] = dispatch
    send(sent_ref, [dot(spread(dispatch, images), rows_ref[...], 1, 0)], [dot(spread(combine, images), grads_ref[...], 1, 0)])


def send(sent_ref, forward, backward):
    groups, hidden, images, width = sent_ref.shape
    width //= 2
    for half, parts in enumerate((forward, backward)):
        parts = [part.astype(bf16).reshape(groups, images, width) for part in parts]
        for index in range(hidden):
            sent_ref[:, index, :, half * width : (half + 1) * width] = parts[index % len(parts)]


def expert_kernel(came_ref, win_ref, bin_ref, wout_ref, bout_ref, sent_ref):
    groups, hidden, images, width = came_ref.shape
    came = [came_ref[:, index].reshape(groups * images, width) for index in range(hidden)]
    width //= 2
    forward = jnp.concatenate([part[:, :width] for part in came], axis=1)
    backward = jnp.concatenate([part[:, width:] for part in came], axis=1)
    activated, slope = gelu_parts(dot(forward, win_ref[...], 1, 0) + bin_ref[...].astype(f32))
    hidden_grad = dot(backward, wout_ref[...], 1, 1)
    out = dot(activated.astype(bf16), wout_ref[...], 1, 0) + bout_ref[...]
    back = dot((hidden_grad * slope).astype(bf16), win_ref[...], 1, 1)
    parts = [slice(index * width, (index + 1) * width) for index in range(hidden)]
    send(sent_ref, [out[:, part] for part in parts], [back[:, part] for part in parts])


def gradient_kernel(came_ref, rows_ref, grads_ref, dispatch_ref, combine_ref, out_ref, back_ref, part_ref):
    slots, hidden, images, width = came_ref.shape
    came = came_ref[:, 0].astype(f32)
    for index in range(1, hidden):
        came = came + came_ref[:, index].astype(f32)
    came = came.astype(bf16).reshape(slots * images, width)
    out, back = came[:, : width // 2], came[:, width // 2 :]
    out_ref[...], back_ref[...] = out, back
    combine_grad = gather(dot(out, grads_ref[...], 1, 1), images)
    dispatch_grad = gather(dot(back, rows_ref[...], 1, 1), images)
    combine, dispatch = combine_ref[...], dispatch_ref[...]
    part = combine * (combine_grad - jnp.sum(combine * combine_grad, axis=0, keepdims=True))
    part = part + dispatch * (dispatch_grad - by_image(dispatch * dispatch_grad, images, jnp.sum, 0.0))
    part_ref[...] = part.astype(bf16)


def mixed_kernel(dispatch_ref, combine_ref, total_ref, out_ref, back_ref, mixed_ref, direct_ref, loss_ref):
    images = loss_ref.shape[0]
    mixed_ref[...] = dot(spread(combine_ref[...], images), out_ref[...], 0, 0).astype(bf16).reshape(mixed_ref.shape)
    direct_ref[...] = dot(spread(dispatch_ref[...], images), back_ref[...], 0, 0)
    total = jnp.broadcast_to(total_ref[...], (8, total_ref.shape[1]))
    tokens = loss_ref.shape[1]
    row, token = iota((images * tokens, tokens), 0), iota((images * tokens, tokens), 1)
    for index in range(images):
        pick = jnp.where(row == images * token + index, 1.0, 0.0)
        own = lax.dot_general(
            total, pick, (((1,), (0,)), ((), ())), precision=lax.Precision.HIGHEST, preferred_element_type=f32
        )[:1]
        loss_ref[index : index + 1] = loss_weight * own * own


def token_kernel(count, *refs):
    parts, refs = refs[:count], refs[count:]
    (combine_ref, total_ref, keys_ref, direct_ref, mixed_ref, loss_ref) = refs[:6]
    (out_ref, mixed_out_ref, loss_out_ref, held_ref, sems) = refs[6:]
    copies = load((mixed_ref, loss_ref), (mixed_out_ref, loss_out_ref), sems)
    logit_grad = tree_sum(parts, False) + 2.0 * loss_weight * total_ref[...] * combine_ref[...]
    out = dot(logit_grad.astype(bf16), keys_ref[...], 0, 0) + direct_ref[...]
    held_ref[...] = out.astype(bf16).reshape(held_ref.shape)
    last = pltpu.make_async_copy(held_ref, out_ref, sems.at[2])
    last.start()
    for copy in (*copies, last):
        copy.wait()


def call(kernel, outs, args, name, limit=8, far=(), far_outs=False, scratch=(), cost=None):
    return pl.pallas_call(
        kernel,
        out_shape=outs,
        in_specs=[VMEM] * len(args) + [HBM] * len(far),
        out_specs=[HBM if far_outs else VMEM] * len(outs),
        scratch_shapes=scratch,
        compiler_params=pltpu.CompilerParams(vmem_limit_bytes=limit * MIB),
        cost_estimate=cost,
        name=name,
    )(*args, *(pltpu.with_memory_space_constraint(value, pltpu.HBM) for value in far))


def exchange(value, axis, first):
    size = lax.axis_size(axis)
    return [value] + [
        lax.ppermute(value, axis, [(source, source ^ step) for source in range(size)]) for step in steps(size, first)
    ]


def per_device(tokens, slot_params, weight_in, bias_in, weight_out, bias_out, cotangent):
    images, count, width = tokens.shape
    groups, hidden = lax.axis_size("expert"), lax.axis_size("hidden")
    slots = slot_params.shape[1]
    wide = weight_in.shape[1]
    rows = images * count
    weight_in, weight_out = weight_in[0], weight_out[0]
    by_token = jnp.transpose(tokens, (1, 0, 2))
    grad_by_token = jnp.transpose(cotangent, (1, 0, 2))
    table = pltpu.VMEM((slots, rows), f32)
    row_shape = pltpu.VMEM((rows, width), bf16)
    held_shape = pltpu.VMEM(by_token.shape, bf16)
    sent_shape = pltpu.VMEM((groups, hidden, images, 2 * width), bf16)

    part, token_rows, keys = call(
        logits_kernel,
        [table, row_shape, pltpu.VMEM((slots, width), bf16)],
        (),
        "logits",
        far=(by_token, jnp.transpose(slot_params)),
        scratch=[held_shape, pltpu.SemaphoreType.DMA((2,))],
    )
    grad_rows, bias_out, bias_in, weight_in, weight_out = call(
        lambda *refs: prepare_kernel("hidden", *refs),
        [row_shape, pltpu.VMEM((1, wide), f32), *[pltpu.VMEM(v.shape, bf16) for v in (bias_in, weight_in, weight_out)]],
        (part,),
        "prepare",
        far=(grad_by_token, bias_out, bias_in, weight_in, weight_out),
        scratch=[held_shape, pltpu.VMEM(bias_out.shape, bf16), pltpu.SemaphoreType.DMA((5,))],
    )
    parts = exchange(part, "hidden", True)
    sent, dispatch, combine, total = call(
        lambda *refs: dispatch_kernel(images, hidden, *refs),
        [sent_shape, table, table, pltpu.VMEM((1, rows), f32)],
        (*parts, token_rows, grad_rows),
        "dispatch",
    )

    def to_all(value):
        value = value.reshape(groups * hidden, images, 2 * width)
        value = lax.all_to_all(value, ("expert", "hidden"), split_axis=0, concat_axis=0, tiled=True)
        return value.reshape(groups, hidden, images, 2 * width)

    (sent,) = call(
        expert_kernel,
        [sent_shape],
        (to_all(sent), weight_in, bias_in, weight_out, bias_out),
        "expert",
        24,
    )
    slot_out, in_grad, part = call(
        gradient_kernel,
        [*[pltpu.VMEM((slots * images, width), bf16)] * 2, pltpu.VMEM((slots, rows), bf16)],
        (to_all(sent), token_rows, grad_rows, dispatch, combine),
        "gradient",
    )
    parts = exchange(part, "hidden", False)
    mixed, direct, zloss = call(
        mixed_kernel,
        [held_shape, pltpu.VMEM((rows, width), f32), pltpu.VMEM((images, count), f32)],
        (dispatch, combine, total, slot_out, in_grad),
        "mixed",
    )
    out_shape = jax.ShapeDtypeStruct(by_token.shape, bf16)
    token_grad, mixed, zloss = call(
        lambda *refs: token_kernel(hidden, *refs),
        [out_shape, out_shape, jax.ShapeDtypeStruct((images, count), f32)],
        (*parts, combine, total, keys, direct, mixed, zloss),
        "token_grad",
        far_outs=True,
        scratch=[held_shape, pltpu.SemaphoreType.DMA((3,))],
    )
    return (jnp.transpose(mixed, (1, 0, 2)), jnp.transpose(token_grad, (1, 0, 2)), zloss)


def solution(mesh):
    return jax.shard_map(
        per_device,
        mesh=mesh,
        in_specs=(
            P("expert", None, "hidden"),
            P("hidden", None),
            P("expert", None, "hidden"),
            P("expert", "hidden"),
            P("expert", "hidden", None),
            P("expert", "hidden"),
            P("expert", None, "hidden"),
        ),
        out_specs=(P("expert", None, "hidden"), P("expert", None, "hidden"), P("expert", None)),
        check_vma=False,
    )
```

```python
import jax
import jax.numpy as jnp
from jax import lax
from jax.experimental import pallas as pl
from jax.experimental.pallas import tpu as pltpu
from jax.sharding import PartitionSpec as P

loss_weight = 0.1
f32, bf16 = jnp.float32, jnp.bfloat16
VMEM = pl.BlockSpec(memory_space=pltpu.VMEM)
HBM = pl.BlockSpec(memory_space=pltpu.HBM)
MIB = 1024 * 1024
weight_pieces = 2


def gelu_parts(value):
    factor = 0.7978845608028654
    inner = factor * (value + 0.044715 * value * value * value)
    slope_tanh = jnp.tanh(inner)
    result = 0.5 * value * (1.0 + slope_tanh)
    slope = 0.5 * (1.0 + slope_tanh) + 0.5 * value * (1.0 - slope_tanh * slope_tanh) * factor * (
        1.0 + 3.0 * 0.044715 * value * value
    )
    return (result, slope)


def dot(lhs, rhs, lhs_dim, rhs_dim):
    dims = (((lhs_dim,), (rhs_dim,)), ((), ()))
    return lax.dot_general(lhs, rhs, dims, preferred_element_type=f32)


def modulo(value, size):
    return value & (size - 1) if size & (size - 1) == 0 else lax.rem(value, size)


def iota(shape, dim):
    return lax.broadcasted_iota(jnp.int32, shape, dim)


def same_image(rows, tokens, images):
    return modulo(iota((rows, tokens), 0), images) == modulo(iota((rows, tokens), 1), images)


def spread(values, images):
    slots, tokens = values.shape
    first = images * iota((images * slots, slots), 1)
    row = iota((images * slots, slots), 0)
    pick = jnp.where((row >= first) & (row < first + images), 1.0, 0.0).astype(bf16)
    wide = dot(pick, values.astype(bf16), 1, 0)
    return jnp.where(same_image(images * slots, tokens, images), wide, 0.0).astype(bf16)


def gather(values, images):
    rows, tokens = values.shape
    values = jnp.where(same_image(rows, tokens, images), values, 0.0)
    return jnp.sum(values.reshape(rows // images, images, tokens), axis=1)


def by_image(values, images, reduce, fill):
    image = modulo(iota(values.shape, 1), images)
    result = None
    for index in range(images):
        here = image == index
        part = reduce(jnp.where(here, values, fill), axis=1, keepdims=True)
        result = part if result is None else jnp.where(here, part, result)
    return jnp.broadcast_to(result, values.shape)


def load(sources, targets, sems):
    copies = [pltpu.make_async_copy(*pair, sems.at[k]) for k, pair in enumerate(zip(sources, targets))]
    for copy in copies:
        copy.start()
    return copies


def logits_kernel(tokens_ref, keys_in_ref, part_ref, rows_ref, keys_ref, held_ref, sems):
    tokens, images, width = tokens_ref.shape
    for copy in load((tokens_ref, keys_in_ref), (held_ref, keys_ref), sems):
        copy.wait()
    rows = held_ref[...].reshape(tokens * images, width)
    rows_ref[...] = rows
    part_ref[...] = dot(keys_ref[...], rows, 1, 1)


def prepare_kernel(axis, after_ref, tokens_ref, bout_in_ref, bin_in_ref, wout_in_ref, win_in_ref,
                   rows_ref, bout_ref, bin_ref, wout_ref, win_ref, wout_turned_ref, win_turned_ref,
                   held_ref, held_bout_ref, sems):
    del after_ref
    tokens, images, width = tokens_ref.shape
    pieces = []
    for source, target, turned in (
        (wout_in_ref, wout_ref, wout_turned_ref), (win_in_ref, win_ref, win_turned_ref)
    ):
        step = source.shape[0] // weight_pieces
        pieces += [(source, target, turned, pl.ds(k * step, step)) for k in range(weight_pieces)]
    copies = load(
        (tokens_ref, bout_in_ref, bin_in_ref, *[source.at[part] for source, _, _, part in pieces]),
        (held_ref, held_bout_ref, bin_ref, *[target.at[part] for _, target, _, part in pieces]),
        sems,
    )
    for copy in copies[:3]:
        copy.wait()
    rows_ref[...] = held_ref[...].reshape(tokens * images, width)
    own = lax.axis_index(axis)
    for index in range(bout_ref.shape[1] // width):
        bias = jnp.where(own == index, held_bout_ref[...].astype(f32), 0.0)
        bout_ref[:, index * width : (index + 1) * width] = bias
    for copy, (_, target, turned, part) in zip(copies[3:], pieces):
        copy.wait()
        turned[:, part] = target[part].T


def steps(size, first):
    return [1] + list(range(size - 1, 1, -1)) if first else list(range(1, size))


def tree_sum(refs, first):
    order = [0] + steps(len(refs), first)
    values = [refs[order.index(step)][...].astype(f32) for step in range(len(refs))]
    while len(values) > 1:
        values = [values[k] + values[k + 1] for k in range(0, len(values), 2)]
    return values[0]


def dispatch_kernel(images, count, *refs):
    parts, (rows_ref, grads_ref, sent_ref, dispatch_ref, combine_ref, total_ref) = refs[:count], refs[count:]
    logits = tree_sum(parts, True)
    top = jnp.max(logits, axis=0, keepdims=True)
    powers = jnp.exp(logits - top)
    sums = jnp.sum(powers, axis=0, keepdims=True)
    combine = powers / sums
    total_ref[...] = top + jnp.log(sums)
    powers = jnp.exp(logits - by_image(logits, images, jnp.max, -jnp.inf))
    dispatch = powers / by_image(powers, images, jnp.sum, 0.0)
    combine_ref[...] = combine
    dispatch_ref[...] = dispatch
    send(sent_ref, [dot(spread(dispatch, images), rows_ref[...], 1, 0)], [dot(spread(combine, images), grads_ref[...], 1, 0)])


def send(sent_ref, forward, backward):
    groups, hidden, images, width = sent_ref.shape
    width //= 2
    for half, parts in enumerate((forward, backward)):
        parts = [part.astype(bf16).reshape(groups, images, width) for part in parts]
        for index in range(hidden):
            sent_ref[:, index, :, half * width : (half + 1) * width] = parts[index % len(parts)]


def expert_kernel(came_ref, bout_ref, bin_ref, wout_ref, win_ref, wout_turned_ref, win_turned_ref, sent_ref):
    groups, hidden, images, width = came_ref.shape
    came = [came_ref[:, index].reshape(groups * images, width) for index in range(hidden)]
    width //= 2
    forward = jnp.concatenate([part[:, :width] for part in came], axis=1)
    backward = jnp.concatenate([part[:, width:] for part in came], axis=1)
    activated, slope = gelu_parts(dot(forward, win_ref[...], 1, 0) + bin_ref[...].astype(f32))
    hidden_grad = dot(backward, wout_turned_ref[...], 1, 0)
    out = dot(activated.astype(bf16), wout_ref[...], 1, 0) + bout_ref[...]
    back = dot((hidden_grad * slope).astype(bf16), win_turned_ref[...], 1, 0)
    parts = [slice(index * width, (index + 1) * width) for index in range(hidden)]
    send(sent_ref, [out[:, part] for part in parts], [back[:, part] for part in parts])


def gradient_kernel(came_ref, rows_ref, grads_ref, dispatch_ref, combine_ref, out_ref, back_ref, part_ref):
    slots, hidden, images, width = came_ref.shape
    came = came_ref[:, 0].astype(f32)
    for index in range(1, hidden):
        came = came + came_ref[:, index].astype(f32)
    came = came.astype(bf16).reshape(slots * images, width)
    out, back = came[:, : width // 2], came[:, width // 2 :]
    out_ref[...], back_ref[...] = out, back
    combine_grad = gather(dot(out, grads_ref[...], 1, 1), images)
    dispatch_grad = gather(dot(back, rows_ref[...], 1, 1), images)
    combine, dispatch = combine_ref[...], dispatch_ref[...]
    part = combine * (combine_grad - jnp.sum(combine * combine_grad, axis=0, keepdims=True))
    part = part + dispatch * (dispatch_grad - by_image(dispatch * dispatch_grad, images, jnp.sum, 0.0))
    part_ref[...] = part.astype(bf16)


def mixed_kernel(dispatch_ref, combine_ref, total_ref, out_ref, back_ref, mixed_ref, direct_ref, loss_ref):
    images = loss_ref.shape[0]
    mixed_ref[...] = dot(spread(combine_ref[...], images), out_ref[...], 0, 0).astype(bf16).reshape(mixed_ref.shape)
    direct_ref[...] = dot(spread(dispatch_ref[...], images), back_ref[...], 0, 0)
    total = jnp.broadcast_to(total_ref[...], (8, total_ref.shape[1]))
    tokens = loss_ref.shape[1]
    row, token = iota((images * tokens, tokens), 0), iota((images * tokens, tokens), 1)
    for index in range(images):
        pick = jnp.where(row == images * token + index, 1.0, 0.0)
        own = lax.dot_general(
            total, pick, (((1,), (0,)), ((), ())), precision=lax.Precision.HIGHEST, preferred_element_type=f32
        )[:1]
        loss_ref[index : index + 1] = loss_weight * own * own


def token_kernel(count, *refs):
    parts, refs = refs[:count], refs[count:]
    (combine_ref, total_ref, keys_ref, direct_ref, mixed_ref, loss_ref) = refs[:6]
    (out_ref, mixed_out_ref, loss_out_ref, held_ref, sems) = refs[6:]
    copies = load((mixed_ref, loss_ref), (mixed_out_ref, loss_out_ref), sems)
    logit_grad = tree_sum(parts, False) + 2.0 * loss_weight * total_ref[...] * combine_ref[...]
    out = dot(logit_grad.astype(bf16), keys_ref[...], 0, 0) + direct_ref[...]
    held_ref[...] = out.astype(bf16).reshape(held_ref.shape)
    last = pltpu.make_async_copy(held_ref, out_ref, sems.at[2])
    last.start()
    for copy in (*copies, last):
        copy.wait()


def call(kernel, outs, args, name, limit=8, far=(), far_outs=False, scratch=(), cost=None):
    return pl.pallas_call(
        kernel,
        out_shape=outs,
        in_specs=[VMEM] * len(args) + [HBM] * len(far),
        out_specs=[HBM if far_outs else VMEM] * len(outs),
        scratch_shapes=scratch,
        compiler_params=pltpu.CompilerParams(vmem_limit_bytes=limit * MIB),
        cost_estimate=cost,
        name=name,
    )(*args, *(pltpu.with_memory_space_constraint(value, pltpu.HBM) for value in far))


def exchange(value, axis, first):
    size = lax.axis_size(axis)
    return [value] + [
        lax.ppermute(value, axis, [(source, source ^ step) for source in range(size)]) for step in steps(size, first)
    ]


def per_device(tokens, slot_params, weight_in, bias_in, weight_out, bias_out, cotangent):
    images, count, width = tokens.shape
    groups, hidden = lax.axis_size("expert"), lax.axis_size("hidden")
    slots = slot_params.shape[1]
    wide = weight_in.shape[1]
    rows = images * count
    weight_in, weight_out = weight_in[0], weight_out[0]
    by_token = jnp.transpose(tokens, (1, 0, 2))
    grad_by_token = jnp.transpose(cotangent, (1, 0, 2))
    table = pltpu.VMEM((slots, rows), f32)
    row_shape = pltpu.VMEM((rows, width), bf16)
    held_shape = pltpu.VMEM(by_token.shape, bf16)
    sent_shape = pltpu.VMEM((groups, hidden, images, 2 * width), bf16)

    part, token_rows, keys = call(
        logits_kernel,
        [table, row_shape, pltpu.VMEM((slots, width), bf16)],
        (),
        "logits",
        far=(by_token, jnp.transpose(slot_params)),
        scratch=[held_shape, pltpu.SemaphoreType.DMA((2,))],
    )
    grad_rows, *expert_values = call(
        lambda *refs: prepare_kernel("hidden", *refs),
        [
            row_shape,
            pltpu.VMEM((1, wide), f32),
            *[pltpu.VMEM(value.shape, bf16) for value in (bias_in, weight_out, weight_in)],
            *[pltpu.VMEM(value.shape[::-1], bf16) for value in (weight_out, weight_in)],
        ],
        (part,),
        "prepare",
        far=(grad_by_token, bias_out, bias_in, weight_out, weight_in),
        scratch=[
            held_shape,
            pltpu.VMEM(bias_out.shape, bf16),
            pltpu.SemaphoreType.DMA((3 + 2 * weight_pieces,)),
        ],
    )
    parts = exchange(part, "hidden", True)
    sent, dispatch, combine, total = call(
        lambda *refs: dispatch_kernel(images, hidden, *refs),
        [sent_shape, table, table, pltpu.VMEM((1, rows), f32)],
        (*parts, token_rows, grad_rows),
        "dispatch",
    )

    def to_all(value):
        value = value.reshape(groups * hidden, images, 2 * width)
        value = lax.all_to_all(value, ("expert", "hidden"), split_axis=0, concat_axis=0, tiled=True)
        return value.reshape(groups, hidden, images, 2 * width)

    (sent,) = call(
        expert_kernel,
        [sent_shape],
        (to_all(sent), *expert_values),
        "expert",
        24,
    )
    slot_out, in_grad, part = call(
        gradient_kernel,
        [*[pltpu.VMEM((slots * images, width), bf16)] * 2, pltpu.VMEM((slots, rows), bf16)],
        (to_all(sent), token_rows, grad_rows, dispatch, combine),
        "gradient",
    )
    parts = exchange(part, "hidden", False)
    mixed, direct, zloss = call(
        mixed_kernel,
        [held_shape, pltpu.VMEM((rows, width), f32), pltpu.VMEM((images, count), f32)],
        (dispatch, combine, total, slot_out, in_grad),
        "mixed",
    )
    out_shape = jax.ShapeDtypeStruct(by_token.shape, bf16)
    token_grad, mixed, zloss = call(
        lambda *refs: token_kernel(hidden, *refs),
        [out_shape, out_shape, jax.ShapeDtypeStruct((images, count), f32)],
        (*parts, combine, total, keys, direct, mixed, zloss),
        "token_grad",
        far_outs=True,
        scratch=[held_shape, pltpu.SemaphoreType.DMA((3,))],
    )
    return (jnp.transpose(mixed, (1, 0, 2)), jnp.transpose(token_grad, (1, 0, 2)), zloss)


def solution(mesh):
    return jax.shard_map(
        per_device,
        mesh=mesh,
        in_specs=(
            P("expert", None, "hidden"),
            P("hidden", None),
            P("expert", None, "hidden"),
            P("expert", "hidden"),
            P("expert", "hidden", None),
            P("expert", "hidden"),
            P("expert", None, "hidden"),
        ),
        out_specs=(P("expert", None, "hidden"), P("expert", None, "hidden"), P("expert", None)),
        check_vma=False,
    )
```

```python
import jax
import jax.numpy as jnp
from jax import lax
from jax.experimental import pallas as pl
from jax.experimental.pallas import tpu as pltpu
from jax.sharding import PartitionSpec as P

loss_weight = 0.1
f32, bf16 = jnp.float32, jnp.bfloat16
VMEM = pl.BlockSpec(memory_space=pltpu.VMEM)
HBM = pl.BlockSpec(memory_space=pltpu.HBM)
MIB = 1024 * 1024
expert = ("expert_a", "expert_b", "expert_c")
send_order = ("expert_a", "expert_c", "expert_b", "hidden")
weight_pieces = 2


def gelu_parts(value):
    factor = 0.7978845608028654
    inner = factor * (value + 0.044715 * value * value * value)
    slope_tanh = jnp.tanh(inner)
    result = 0.5 * value * (1.0 + slope_tanh)
    slope = 0.5 * (1.0 + slope_tanh) + 0.5 * value * (1.0 - slope_tanh * slope_tanh) * factor * (
        1.0 + 3.0 * 0.044715 * value * value
    )
    return (result, slope)


def dot(lhs, rhs, lhs_dim, rhs_dim):
    dims = (((lhs_dim,), (rhs_dim,)), ((), ()))
    return lax.dot_general(lhs, rhs, dims, preferred_element_type=f32)


def modulo(value, size):
    return value & (size - 1) if size & (size - 1) == 0 else lax.rem(value, size)


def iota(shape, dim):
    return lax.broadcasted_iota(jnp.int32, shape, dim)


def same_image(rows, tokens, images):
    return modulo(iota((rows, tokens), 0), images) == modulo(iota((rows, tokens), 1), images)


def spread(values, images):
    slots, tokens = values.shape
    first = images * iota((images * slots, slots), 1)
    row = iota((images * slots, slots), 0)
    pick = jnp.where((row >= first) & (row < first + images), 1.0, 0.0).astype(bf16)
    wide = dot(pick, values.astype(bf16), 1, 0)
    return jnp.where(same_image(images * slots, tokens, images), wide, 0.0).astype(bf16)


def gather(values, images):
    rows, tokens = values.shape
    values = jnp.where(same_image(rows, tokens, images), values, 0.0)
    return jnp.sum(values.reshape(rows // images, images, tokens), axis=1)


def by_image(values, images, reduce, fill):
    image = modulo(iota(values.shape, 1), images)
    result = None
    for index in range(images):
        here = image == index
        part = reduce(jnp.where(here, values, fill), axis=1, keepdims=True)
        result = part if result is None else jnp.where(here, part, result)
    return jnp.broadcast_to(result, values.shape)


def load(sources, targets, sems):
    copies = [pltpu.make_async_copy(*pair, sems.at[k]) for k, pair in enumerate(zip(sources, targets))]
    for copy in copies:
        copy.start()
    return copies


def in_turn(keys, halves):
    slots = keys.shape[0]
    middle = slots // (halves * halves)
    to, source = iota((slots, slots), 0), iota((slots, slots), 1)
    pick = jnp.zeros((slots, slots), f32)
    for a in range(halves):
        for c in range(halves):
            b = to - (a * halves + c) * middle
            here = (b >= 0) & (b < middle) & (source == (a * middle + b) * halves + c)
            pick = jnp.where(here, 1.0, pick)
    return dot(pick.astype(bf16), keys, 1, 0).astype(bf16)


def logits_kernel(halves, tokens_ref, keys_in_ref, part_ref, rows_ref, keys_ref, held_ref, held_keys_ref, sems):
    tokens, images, width = tokens_ref.shape
    copies = load((tokens_ref, keys_in_ref), (held_ref, held_keys_ref), sems)
    copies[1].wait()
    keys_ref[...] = in_turn(held_keys_ref[...], halves)
    copies[0].wait()
    rows = held_ref[...].reshape(tokens * images, width)
    rows_ref[...] = rows
    part_ref[...] = dot(keys_ref[...], rows, 1, 1)


def prepare_kernel(axis, after_ref, tokens_ref, bout_in_ref, bin_in_ref, wout_in_ref, win_in_ref,
                   rows_ref, bout_ref, bin_ref, wout_ref, win_ref, wout_turned_ref, win_turned_ref,
                   held_ref, held_bout_ref, sems):
    del after_ref
    tokens, images, width = tokens_ref.shape
    pieces = []
    for source, target, turned in (
        (wout_in_ref, wout_ref, wout_turned_ref), (win_in_ref, win_ref, win_turned_ref)
    ):
        step = source.shape[0] // weight_pieces
        pieces += [(source, target, turned, pl.ds(k * step, step)) for k in range(weight_pieces)]
    copies = load(
        (tokens_ref, bout_in_ref, bin_in_ref, *[source.at[part] for source, _, _, part in pieces]),
        (held_ref, held_bout_ref, bin_ref, *[target.at[part] for _, target, _, part in pieces]),
        sems,
    )
    for copy in copies[:3]:
        copy.wait()
    rows_ref[...] = held_ref[...].reshape(tokens * images, width)
    own = lax.axis_index(axis)
    for index in range(bout_ref.shape[1] // width):
        bias = jnp.where(own == index, held_bout_ref[...].astype(f32), 0.0)
        bout_ref[:, index * width : (index + 1) * width] = bias
    for copy, (_, target, turned, part) in zip(copies[3:], pieces):
        copy.wait()
        turned[:, part] = target[part].T


def steps(size, first):
    return [1] + list(range(size - 1, 1, -1)) if first else list(range(1, size))


def tree_sum(refs, first):
    order = [0] + steps(len(refs), first)
    values = [refs[order.index(step)][...].astype(f32) for step in range(len(refs))]
    while len(values) > 1:
        values = [values[k] + values[k + 1] for k in range(0, len(values), 2)]
    return values[0]


def dispatch_kernel(images, count, *refs):
    parts, (rows_ref, grads_ref, sent_ref, dispatch_ref, combine_ref, total_ref) = refs[:count], refs[count:]
    logits = tree_sum(parts, True)
    top = jnp.max(logits, axis=0, keepdims=True)
    powers = jnp.exp(logits - top)
    sums = jnp.sum(powers, axis=0, keepdims=True)
    combine = powers / sums
    total_ref[...] = top + jnp.log(sums)
    powers = jnp.exp(logits - by_image(logits, images, jnp.max, -jnp.inf))
    dispatch = powers / by_image(powers, images, jnp.sum, 0.0)
    combine_ref[...] = combine
    dispatch_ref[...] = dispatch
    send(sent_ref, [dot(spread(dispatch, images), rows_ref[...], 1, 0)], [dot(spread(combine, images), grads_ref[...], 1, 0)])


def send(sent_ref, forward, backward):
    groups, hidden, images, width = sent_ref.shape
    width //= 2
    for half, parts in enumerate((forward, backward)):
        parts = [part.astype(bf16).reshape(groups, images, width) for part in parts]
        for index in range(hidden):
            sent_ref[:, index, :, half * width : (half + 1) * width] = parts[index % len(parts)]


def expert_kernel(came_ref, bout_ref, bin_ref, wout_ref, win_ref, wout_turned_ref, win_turned_ref, sent_ref):
    groups, hidden, images, width = came_ref.shape
    came = [came_ref[:, index].reshape(groups * images, width) for index in range(hidden)]
    width //= 2
    forward = jnp.concatenate([part[:, :width] for part in came], axis=1)
    backward = jnp.concatenate([part[:, width:] for part in came], axis=1)
    activated, slope = gelu_parts(dot(forward, win_ref[...], 1, 0) + bin_ref[...].astype(f32))
    hidden_grad = dot(backward, wout_turned_ref[...], 1, 0)
    out = dot(activated.astype(bf16), wout_ref[...], 1, 0) + bout_ref[...]
    back = dot((hidden_grad * slope).astype(bf16), win_turned_ref[...], 1, 0)
    parts = [slice(index * width, (index + 1) * width) for index in range(hidden)]
    send(sent_ref, [out[:, part] for part in parts], [back[:, part] for part in parts])


def gradient_kernel(came_ref, rows_ref, grads_ref, dispatch_ref, combine_ref, out_ref, back_ref, part_ref):
    slots, hidden, images, width = came_ref.shape
    came = came_ref[:, 0].astype(f32)
    for index in range(1, hidden):
        came = came + came_ref[:, index].astype(f32)
    came = came.astype(bf16).reshape(slots * images, width)
    out, back = came[:, : width // 2], came[:, width // 2 :]
    out_ref[...], back_ref[...] = out, back
    combine_grad = gather(dot(out, grads_ref[...], 1, 1), images)
    dispatch_grad = gather(dot(back, rows_ref[...], 1, 1), images)
    combine, dispatch = combine_ref[...], dispatch_ref[...]
    part = combine * (combine_grad - jnp.sum(combine * combine_grad, axis=0, keepdims=True))
    part = part + dispatch * (dispatch_grad - by_image(dispatch * dispatch_grad, images, jnp.sum, 0.0))
    part_ref[...] = part.astype(bf16)


def mixed_kernel(dispatch_ref, combine_ref, total_ref, out_ref, back_ref, mixed_ref, direct_ref, loss_ref):
    images = loss_ref.shape[0]
    mixed_ref[...] = dot(spread(combine_ref[...], images), out_ref[...], 0, 0).astype(bf16).reshape(mixed_ref.shape)
    direct_ref[...] = dot(spread(dispatch_ref[...], images), back_ref[...], 0, 0)
    total = jnp.broadcast_to(total_ref[...], (8, total_ref.shape[1]))
    tokens = loss_ref.shape[1]
    row, token = iota((images * tokens, tokens), 0), iota((images * tokens, tokens), 1)
    for index in range(images):
        pick = jnp.where(row == images * token + index, 1.0, 0.0)
        own = lax.dot_general(
            total, pick, (((1,), (0,)), ((), ())), precision=lax.Precision.HIGHEST, preferred_element_type=f32
        )[:1]
        loss_ref[index : index + 1] = loss_weight * own * own


def token_kernel(count, *refs):
    parts, refs = refs[:count], refs[count:]
    (combine_ref, total_ref, keys_ref, direct_ref, mixed_ref, loss_ref) = refs[:6]
    (out_ref, mixed_out_ref, loss_out_ref, held_ref, sems) = refs[6:]
    copies = load((mixed_ref, loss_ref), (mixed_out_ref, loss_out_ref), sems)
    logit_grad = tree_sum(parts, False) + 2.0 * loss_weight * total_ref[...] * combine_ref[...]
    out = dot(logit_grad.astype(bf16), keys_ref[...], 0, 0) + direct_ref[...]
    held_ref[...] = out.astype(bf16).reshape(held_ref.shape)
    last = pltpu.make_async_copy(held_ref, out_ref, sems.at[2])
    last.start()
    for copy in (*copies, last):
        copy.wait()


def call(kernel, outs, args, name, limit=8, far=(), far_outs=False, scratch=(), cost=None):
    return pl.pallas_call(
        kernel,
        out_shape=outs,
        in_specs=[VMEM] * len(args) + [HBM] * len(far),
        out_specs=[HBM if far_outs else VMEM] * len(outs),
        scratch_shapes=scratch,
        compiler_params=pltpu.CompilerParams(vmem_limit_bytes=limit * MIB),
        cost_estimate=cost,
        name=name,
    )(*args, *(pltpu.with_memory_space_constraint(value, pltpu.HBM) for value in far))


def exchange(value, axis, first):
    size = lax.axis_size(axis)
    return [value] + [
        lax.ppermute(value, axis, [(source, source ^ step) for source in range(size)]) for step in steps(size, first)
    ]


def per_device(tokens, slot_params, weight_in, bias_in, weight_out, bias_out, cotangent):
    images, count, width = tokens.shape
    groups, hidden = lax.axis_size(expert), lax.axis_size("hidden")
    slots = slot_params.shape[1]
    wide = weight_in.shape[1]
    rows = images * count
    weight_in, weight_out = weight_in[0], weight_out[0]
    by_token = jnp.transpose(tokens, (1, 0, 2))
    grad_by_token = jnp.transpose(cotangent, (1, 0, 2))
    table = pltpu.VMEM((slots, rows), f32)
    row_shape = pltpu.VMEM((rows, width), bf16)
    held_shape = pltpu.VMEM(by_token.shape, bf16)
    sent_shape = pltpu.VMEM((groups, hidden, images, 2 * width), bf16)

    part, token_rows, keys = call(
        lambda *refs: logits_kernel(lax.axis_size("expert_c"), *refs),
        [table, row_shape, pltpu.VMEM((slots, width), bf16)],
        (),
        "logits",
        far=(by_token, jnp.transpose(slot_params)),
        scratch=[held_shape, pltpu.VMEM((slots, width), bf16), pltpu.SemaphoreType.DMA((2,))],
    )
    grad_rows, *expert_values = call(
        lambda *refs: prepare_kernel("hidden", *refs),
        [
            row_shape,
            pltpu.VMEM((1, wide), f32),
            *[pltpu.VMEM(value.shape, bf16) for value in (bias_in, weight_out, weight_in)],
            *[pltpu.VMEM(value.shape[::-1], bf16) for value in (weight_out, weight_in)],
        ],
        (part,),
        "prepare",
        far=(grad_by_token, bias_out, bias_in, weight_out, weight_in),
        scratch=[
            held_shape,
            pltpu.VMEM(bias_out.shape, bf16),
            pltpu.SemaphoreType.DMA((3 + 2 * weight_pieces,)),
        ],
    )
    parts = exchange(part, "hidden", True)
    sent, dispatch, combine, total = call(
        lambda *refs: dispatch_kernel(images, hidden, *refs),
        [sent_shape, table, table, pltpu.VMEM((1, rows), f32)],
        (*parts, token_rows, grad_rows),
        "dispatch",
    )

    def to_all(value):
        value = value.reshape(groups * hidden, images, 2 * width)
        value = lax.all_to_all(value, send_order, split_axis=0, concat_axis=0, tiled=True)
        return value.reshape(groups, hidden, images, 2 * width)

    (sent,) = call(
        expert_kernel,
        [sent_shape],
        (to_all(sent), *expert_values),
        "expert",
        24,
    )
    slot_out, in_grad, part = call(
        gradient_kernel,
        [*[pltpu.VMEM((slots * images, width), bf16)] * 2, pltpu.VMEM((slots, rows), bf16)],
        (to_all(sent), token_rows, grad_rows, dispatch, combine),
        "gradient",
    )
    parts = exchange(part, "hidden", False)
    mixed, direct, zloss = call(
        mixed_kernel,
        [held_shape, pltpu.VMEM((rows, width), f32), pltpu.VMEM((images, count), f32)],
        (dispatch, combine, total, slot_out, in_grad),
        "mixed",
    )
    out_shape = jax.ShapeDtypeStruct(by_token.shape, bf16)
    token_grad, mixed, zloss = call(
        lambda *refs: token_kernel(hidden, *refs),
        [out_shape, out_shape, jax.ShapeDtypeStruct((images, count), f32)],
        (*parts, combine, total, keys, direct, mixed, zloss),
        "token_grad",
        far_outs=True,
        scratch=[held_shape, pltpu.SemaphoreType.DMA((3,))],
    )
    return (jnp.transpose(mixed, (1, 0, 2)), jnp.transpose(token_grad, (1, 0, 2)), zloss)


def solution(mesh):
    groups, hidden = mesh.devices.shape
    halves = 2 if groups % 4 == 0 else 1
    parts = (halves, groups // (halves * halves), halves, hidden)
    return jax.shard_map(
        per_device,
        mesh=jax.sharding.Mesh(mesh.devices.reshape(parts), (*expert, "hidden")),
        in_specs=(
            P(expert, None, "hidden"),
            P("hidden", None),
            P(expert, None, "hidden"),
            P(expert, "hidden"),
            P(expert, "hidden", None),
            P(expert, "hidden"),
            P(expert, None, "hidden"),
        ),
        out_specs=(P(expert, None, "hidden"), P(expert, None, "hidden"), P(expert, None)),
        check_vma=False,
    )
```

```python
import jax
import jax.numpy as jnp
from jax import lax
from jax.experimental import pallas as pl
from jax.experimental.pallas import tpu as pltpu
from jax.sharding import PartitionSpec as P

loss_weight = 0.1
f32, bf16 = jnp.float32, jnp.bfloat16
VMEM = pl.BlockSpec(memory_space=pltpu.VMEM)
HBM = pl.BlockSpec(memory_space=pltpu.HBM)
MIB = 1024 * 1024
expert = ("expert_a", "expert_b", "expert_c")
send_order = ("expert_a", "expert_c", "expert_b", "hidden")
weight_pieces = 2


def gelu_parts(value):
    factor = 0.7978845608028654
    inner = factor * (value + 0.044715 * value * value * value)
    slope_tanh = jnp.tanh(inner)
    result = 0.5 * value * (1.0 + slope_tanh)
    slope = 0.5 * (1.0 + slope_tanh) + 0.5 * value * (1.0 - slope_tanh * slope_tanh) * factor * (
        1.0 + 3.0 * 0.044715 * value * value
    )
    return (result, slope)


def dot(lhs, rhs, lhs_dim, rhs_dim):
    dims = (((lhs_dim,), (rhs_dim,)), ((), ()))
    return lax.dot_general(lhs, rhs, dims, preferred_element_type=f32)


def modulo(value, size):
    return value & (size - 1) if size & (size - 1) == 0 else lax.rem(value, size)


def iota(shape, dim):
    return lax.broadcasted_iota(jnp.int32, shape, dim)


def same_image(rows, tokens, images):
    return modulo(iota((rows, tokens), 0), images) == modulo(iota((rows, tokens), 1), images)


def spread(values, images):
    slots, tokens = values.shape
    first = images * iota((images * slots, slots), 1)
    row = iota((images * slots, slots), 0)
    pick = jnp.where((row >= first) & (row < first + images), 1.0, 0.0).astype(bf16)
    wide = dot(pick, values.astype(bf16), 1, 0)
    return jnp.where(same_image(images * slots, tokens, images), wide, 0.0).astype(bf16)


def gather(values, images):
    rows, tokens = values.shape
    values = jnp.where(same_image(rows, tokens, images), values, 0.0)
    return jnp.sum(values.reshape(rows // images, images, tokens), axis=1)


def by_image(values, images, reduce, fill):
    image = modulo(iota(values.shape, 1), images)
    result = None
    for index in range(images):
        here = image == index
        part = reduce(jnp.where(here, values, fill), axis=1, keepdims=True)
        result = part if result is None else jnp.where(here, part, result)
    return jnp.broadcast_to(result, values.shape)


def load(sources, targets, sems):
    copies = [pltpu.make_async_copy(*pair, sems.at[k]) for k, pair in enumerate(zip(sources, targets))]
    for copy in copies:
        copy.start()
    return copies


def in_turn(keys, halves):
    slots = keys.shape[0]
    middle = slots // (halves * halves)
    to, source = iota((slots, slots), 0), iota((slots, slots), 1)
    pick = jnp.zeros((slots, slots), f32)
    for a in range(halves):
        for c in range(halves):
            b = to - (a * halves + c) * middle
            here = (b >= 0) & (b < middle) & (source == (a * middle + b) * halves + c)
            pick = jnp.where(here, 1.0, pick)
    return dot(pick.astype(bf16), keys, 1, 0).astype(bf16)


def logits_kernel(halves, tokens_ref, keys_in_ref, part_ref, rows_ref, keys_ref, held_ref, held_keys_ref, sems):
    tokens, images, width = tokens_ref.shape
    copies = load((tokens_ref, keys_in_ref), (held_ref, held_keys_ref), sems)
    copies[1].wait()
    keys_ref[...] = in_turn(held_keys_ref[...], halves)
    copies[0].wait()
    rows = held_ref[...].reshape(tokens * images, width)
    rows_ref[...] = rows
    part_ref[...] = dot(keys_ref[...], rows, 1, 1)


def prepare_kernel(axis, after_ref, tokens_ref, bout_in_ref, bin_in_ref, wout_in_ref, win_in_ref,
                   rows_ref, bout_ref, bin_ref, wout_ref, win_ref, wout_turned_ref, win_turned_ref,
                   held_ref, held_bout_ref, sems):
    del after_ref
    tokens, images, width = tokens_ref.shape
    pieces = []
    for source, target, turned in (
        (wout_in_ref, wout_ref, wout_turned_ref), (win_in_ref, win_ref, win_turned_ref)
    ):
        step = source.shape[0] // weight_pieces
        pieces += [(source, target, turned, pl.ds(k * step, step)) for k in range(weight_pieces)]
    copies = load(
        (tokens_ref, bout_in_ref, bin_in_ref, *[source.at[part] for source, _, _, part in pieces]),
        (held_ref, held_bout_ref, bin_ref, *[target.at[part] for _, target, _, part in pieces]),
        sems,
    )
    for copy in copies[:3]:
        copy.wait()
    rows_ref[...] = held_ref[...].reshape(tokens * images, width)
    own = lax.axis_index(axis)
    for index in range(bout_ref.shape[1] // width):
        bias = jnp.where(own == index, held_bout_ref[...].astype(f32), 0.0)
        bout_ref[:, index * width : (index + 1) * width] = bias
    for copy, (_, target, turned, part) in zip(copies[3:], pieces):
        copy.wait()
        turned[:, part] = target[part].T


def steps(size, first):
    return list(range(2, size)) + [1] if first else list(range(1, size))


def tree_sum(refs, first):
    order = [0] + steps(len(refs), first)
    values = [refs[order.index(step)][...].astype(f32) for step in range(len(refs))]
    while len(values) > 1:
        values = [values[k] + values[k + 1] for k in range(0, len(values), 2)]
    return values[0]


def dispatch_kernel(images, count, *refs):
    parts, (rows_ref, grads_ref, sent_ref, dispatch_ref, combine_ref, total_ref) = refs[:count], refs[count:]
    logits = tree_sum(parts, True)
    top = jnp.max(logits, axis=0, keepdims=True)
    powers = jnp.exp(logits - top)
    sums = jnp.sum(powers, axis=0, keepdims=True)
    combine = powers / sums
    total_ref[...] = top + jnp.log(sums)
    powers = jnp.exp(logits - by_image(logits, images, jnp.max, -jnp.inf))
    dispatch = powers / by_image(powers, images, jnp.sum, 0.0)
    combine_ref[...] = combine
    dispatch_ref[...] = dispatch
    send(sent_ref, [dot(spread(dispatch, images), rows_ref[...], 1, 0)], [dot(spread(combine, images), grads_ref[...], 1, 0)])


def send(sent_ref, forward, backward):
    groups, hidden, images, width = sent_ref.shape
    width //= 2
    for half, parts in enumerate((forward, backward)):
        parts = [part.astype(bf16).reshape(groups, images, width) for part in parts]
        for index in range(hidden):
            sent_ref[:, index, :, half * width : (half + 1) * width] = parts[index % len(parts)]


def expert_kernel(came_ref, bout_ref, bin_ref, wout_ref, win_ref, wout_turned_ref, win_turned_ref, sent_ref):
    groups, hidden, images, width = came_ref.shape
    came = [came_ref[:, index].reshape(groups * images, width) for index in range(hidden)]
    width //= 2
    forward = jnp.concatenate([part[:, :width] for part in came], axis=1)
    backward = jnp.concatenate([part[:, width:] for part in came], axis=1)
    activated, slope = gelu_parts(dot(forward, win_ref[...], 1, 0) + bin_ref[...].astype(f32))
    hidden_grad = dot(backward, wout_turned_ref[...], 1, 0)
    out = dot(activated.astype(bf16), wout_ref[...], 1, 0) + bout_ref[...]
    back = dot((hidden_grad * slope).astype(bf16), win_turned_ref[...], 1, 0)
    parts = [slice(index * width, (index + 1) * width) for index in range(hidden)]
    send(sent_ref, [out[:, part] for part in parts], [back[:, part] for part in parts])


def gradient_kernel(came_ref, rows_ref, grads_ref, dispatch_ref, combine_ref, out_ref, back_ref, part_ref):
    slots, hidden, images, width = came_ref.shape
    came = came_ref[:, 0].astype(f32)
    for index in range(1, hidden):
        came = came + came_ref[:, index].astype(f32)
    came = came.astype(bf16).reshape(slots * images, width)
    out, back = came[:, : width // 2], came[:, width // 2 :]
    out_ref[...], back_ref[...] = out, back
    combine_grad = gather(dot(out, grads_ref[...], 1, 1), images)
    dispatch_grad = gather(dot(back, rows_ref[...], 1, 1), images)
    combine, dispatch = combine_ref[...], dispatch_ref[...]
    part = combine * (combine_grad - jnp.sum(combine * combine_grad, axis=0, keepdims=True))
    part = part + dispatch * (dispatch_grad - by_image(dispatch * dispatch_grad, images, jnp.sum, 0.0))
    part_ref[...] = part.astype(bf16)


def mixed_kernel(dispatch_ref, combine_ref, total_ref, out_ref, back_ref, mixed_ref, direct_ref, loss_ref):
    images = loss_ref.shape[0]
    mixed_ref[...] = dot(spread(combine_ref[...], images), out_ref[...], 0, 0).astype(bf16).reshape(mixed_ref.shape)
    direct_ref[...] = dot(spread(dispatch_ref[...], images), back_ref[...], 0, 0)
    total = jnp.broadcast_to(total_ref[...], (8, total_ref.shape[1]))
    tokens = loss_ref.shape[1]
    row, token = iota((images * tokens, tokens), 0), iota((images * tokens, tokens), 1)
    for index in range(images):
        pick = jnp.where(row == images * token + index, 1.0, 0.0)
        own = lax.dot_general(
            total, pick, (((1,), (0,)), ((), ())), precision=lax.Precision.HIGHEST, preferred_element_type=f32
        )[:1]
        loss_ref[index : index + 1] = loss_weight * own * own


def token_kernel(count, *refs):
    parts, refs = refs[:count], refs[count:]
    (combine_ref, total_ref, keys_ref, direct_ref, mixed_ref, loss_ref) = refs[:6]
    (out_ref, mixed_out_ref, loss_out_ref, held_ref, sems) = refs[6:]
    copies = load((mixed_ref, loss_ref), (mixed_out_ref, loss_out_ref), sems)
    logit_grad = tree_sum(parts, False) + 2.0 * loss_weight * total_ref[...] * combine_ref[...]
    out = dot(logit_grad.astype(bf16), keys_ref[...], 0, 0) + direct_ref[...]
    held_ref[...] = out.astype(bf16).reshape(held_ref.shape)
    last = pltpu.make_async_copy(held_ref, out_ref, sems.at[2])
    last.start()
    for copy in (*copies, last):
        copy.wait()


def call(kernel, outs, args, name, limit=8, far=(), far_outs=False, scratch=(), cost=None):
    return pl.pallas_call(
        kernel,
        out_shape=outs,
        in_specs=[VMEM] * len(args) + [HBM] * len(far),
        out_specs=[HBM if far_outs else VMEM] * len(outs),
        scratch_shapes=scratch,
        compiler_params=pltpu.CompilerParams(vmem_limit_bytes=limit * MIB),
        cost_estimate=cost,
        name=name,
    )(*args, *(pltpu.with_memory_space_constraint(value, pltpu.HBM) for value in far))


def exchange(value, axis, first):
    size = lax.axis_size(axis)
    return [value] + [
        lax.ppermute(value, axis, [(source, source ^ step) for source in range(size)]) for step in steps(size, first)
    ]


def per_device(tokens, slot_params, weight_in, bias_in, weight_out, bias_out, cotangent):
    images, count, width = tokens.shape
    groups, hidden = lax.axis_size(expert), lax.axis_size("hidden")
    slots = slot_params.shape[1]
    wide = weight_in.shape[1]
    rows = images * count
    weight_in, weight_out = weight_in[0], weight_out[0]
    by_token = jnp.transpose(tokens, (1, 0, 2))
    grad_by_token = jnp.transpose(cotangent, (1, 0, 2))
    table = pltpu.VMEM((slots, rows), f32)
    row_shape = pltpu.VMEM((rows, width), bf16)
    held_shape = pltpu.VMEM(by_token.shape, bf16)
    sent_shape = pltpu.VMEM((groups, hidden, images, 2 * width), bf16)

    part, token_rows, keys = call(
        lambda *refs: logits_kernel(lax.axis_size("expert_c"), *refs),
        [table, row_shape, pltpu.VMEM((slots, width), bf16)],
        (),
        "logits",
        far=(by_token, jnp.transpose(slot_params)),
        scratch=[held_shape, pltpu.VMEM((slots, width), bf16), pltpu.SemaphoreType.DMA((2,))],
    )
    grad_rows, *expert_values = call(
        lambda *refs: prepare_kernel("hidden", *refs),
        [
            row_shape,
            pltpu.VMEM((1, wide), f32),
            *[pltpu.VMEM(value.shape, bf16) for value in (bias_in, weight_out, weight_in)],
            *[pltpu.VMEM(value.shape[::-1], bf16) for value in (weight_out, weight_in)],
        ],
        (part,),
        "prepare",
        far=(grad_by_token, bias_out, bias_in, weight_out, weight_in),
        scratch=[
            held_shape,
            pltpu.VMEM(bias_out.shape, bf16),
            pltpu.SemaphoreType.DMA((3 + 2 * weight_pieces,)),
        ],
    )
    parts = exchange(part, "hidden", True)
    sent, dispatch, combine, total = call(
        lambda *refs: dispatch_kernel(images, hidden, *refs),
        [sent_shape, table, table, pltpu.VMEM((1, rows), f32)],
        (*parts, token_rows, grad_rows),
        "dispatch",
    )

    def to_all(value):
        value = value.reshape(groups * hidden, images, 2 * width)
        value = lax.all_to_all(value, send_order, split_axis=0, concat_axis=0, tiled=True)
        return value.reshape(groups, hidden, images, 2 * width)

    (sent,) = call(
        expert_kernel,
        [sent_shape],
        (to_all(sent), *expert_values),
        "expert",
        24,
    )
    slot_out, in_grad, part = call(
        gradient_kernel,
        [*[pltpu.VMEM((slots * images, width), bf16)] * 2, pltpu.VMEM((slots, rows), bf16)],
        (to_all(sent), token_rows, grad_rows, dispatch, combine),
        "gradient",
    )
    parts = exchange(part, "hidden", False)
    mixed, direct, zloss = call(
        mixed_kernel,
        [held_shape, pltpu.VMEM((rows, width), f32), pltpu.VMEM((images, count), f32)],
        (dispatch, combine, total, slot_out, in_grad),
        "mixed",
    )
    out_shape = jax.ShapeDtypeStruct(by_token.shape, bf16)
    token_grad, mixed, zloss = call(
        lambda *refs: token_kernel(hidden, *refs),
        [out_shape, out_shape, jax.ShapeDtypeStruct((images, count), f32)],
        (*parts, combine, total, keys, direct, mixed, zloss),
        "token_grad",
        far_outs=True,
        scratch=[held_shape, pltpu.SemaphoreType.DMA((3,))],
    )
    return (jnp.transpose(mixed, (1, 0, 2)), jnp.transpose(token_grad, (1, 0, 2)), zloss)


def solution(mesh):
    groups, hidden = mesh.devices.shape
    halves = 2 if groups % 4 == 0 else 1
    parts = (halves, groups // (halves * halves), halves, hidden)
    return jax.shard_map(
        per_device,
        mesh=jax.sharding.Mesh(mesh.devices.reshape(parts), (*expert, "hidden")),
        in_specs=(
            P(expert, None, "hidden"),
            P("hidden", None),
            P(expert, None, "hidden"),
            P(expert, "hidden"),
            P(expert, "hidden", None),
            P(expert, "hidden"),
            P(expert, None, "hidden"),
        ),
        out_specs=(P(expert, None, "hidden"), P(expert, None, "hidden"), P(expert, None)),
        check_vma=False,
    )
```

```python
import jax
import jax.numpy as jnp
from jax import lax
from jax.experimental import pallas as pl
from jax.experimental.pallas import tpu as pltpu
from jax.sharding import PartitionSpec as P

loss_weight = 0.1
f32, bf16 = jnp.float32, jnp.bfloat16
VMEM = pl.BlockSpec(memory_space=pltpu.VMEM)
HBM = pl.BlockSpec(memory_space=pltpu.HBM)
MIB = 1024 * 1024
expert = ("expert_a", "expert_b", "expert_c")
send_order = ("expert_a", "expert_c", "expert_b", "hidden")
weight_pieces = 2


def gelu_parts(value):
    factor = 0.7978845608028654
    inner = factor * (value + 0.044715 * value * value * value)
    slope_tanh = jnp.tanh(inner)
    result = 0.5 * value * (1.0 + slope_tanh)
    slope = 0.5 * (1.0 + slope_tanh) + 0.5 * value * (1.0 - slope_tanh * slope_tanh) * factor * (
        1.0 + 3.0 * 0.044715 * value * value
    )
    return (result, slope)


def dot(lhs, rhs, lhs_dim, rhs_dim):
    dims = (((lhs_dim,), (rhs_dim,)), ((), ()))
    return lax.dot_general(lhs, rhs, dims, preferred_element_type=f32)


def modulo(value, size):
    return value & (size - 1) if size & (size - 1) == 0 else lax.rem(value, size)


def iota(shape, dim):
    return lax.broadcasted_iota(jnp.int32, shape, dim)


def same_image(rows, tokens, images):
    return modulo(iota((rows, tokens), 0), images) == modulo(iota((rows, tokens), 1), images)


def spread(values, images):
    slots, tokens = values.shape
    first = images * iota((images * slots, slots), 1)
    row = iota((images * slots, slots), 0)
    pick = jnp.where((row >= first) & (row < first + images), 1.0, 0.0).astype(bf16)
    wide = dot(pick, values.astype(bf16), 1, 0)
    return jnp.where(same_image(images * slots, tokens, images), wide, 0.0).astype(bf16)


def gather(values, images):
    rows, tokens = values.shape
    values = jnp.where(same_image(rows, tokens, images), values, 0.0)
    return jnp.sum(values.reshape(rows // images, images, tokens), axis=1)


def by_image(values, images, reduce, fill):
    image = modulo(iota(values.shape, 1), images)
    result = None
    for index in range(images):
        here = image == index
        part = reduce(jnp.where(here, values, fill), axis=1, keepdims=True)
        result = part if result is None else jnp.where(here, part, result)
    return jnp.broadcast_to(result, values.shape)


def load(sources, targets, sems):
    copies = [pltpu.make_async_copy(*pair, sems.at[k]) for k, pair in enumerate(zip(sources, targets))]
    for copy in copies:
        copy.start()
    return copies


def in_turn(keys, halves):
    slots = keys.shape[0]
    middle = slots // (halves * halves)
    to, source = iota((slots, slots), 0), iota((slots, slots), 1)
    pick = jnp.zeros((slots, slots), f32)
    for a in range(halves):
        for c in range(halves):
            b = to - (a * halves + c) * middle
            here = (b >= 0) & (b < middle) & (source == (a * middle + b) * halves + c)
            pick = jnp.where(here, 1.0, pick)
    return dot(pick.astype(bf16), keys, 1, 0).astype(bf16)


def logits_kernel(halves, tokens_ref, keys_in_ref, grads_ref, part_ref, rows_ref, keys_ref, raw_ref, held_ref, held_keys_ref, sems):
    tokens, images, width = tokens_ref.shape
    copies = load((tokens_ref, keys_in_ref, grads_ref), (held_ref, held_keys_ref, raw_ref), sems)
    copies[1].wait()
    keys_ref[...] = in_turn(held_keys_ref[...], halves)
    copies[0].wait()
    rows = held_ref[...].reshape(tokens * images, width)
    rows_ref[...] = rows
    part_ref[...] = dot(keys_ref[...], rows, 1, 1)
    copies[2].wait()


def prepare_kernel(axis, held_ref, bout_in_ref, bin_in_ref, wout_in_ref, win_in_ref,
                   rows_ref, bout_ref, bin_ref, wout_ref, win_ref, wout_turned_ref, win_turned_ref,
                   held_bout_ref, sems):
    tokens, images, width = held_ref.shape
    pieces = []
    for source, target, turned in (
        (wout_in_ref, wout_ref, wout_turned_ref), (win_in_ref, win_ref, win_turned_ref)
    ):
        step = source.shape[0] // weight_pieces
        pieces += [(source, target, turned, pl.ds(k * step, step)) for k in range(weight_pieces)]
    copies = load(
        (bout_in_ref, bin_in_ref, *[source.at[part] for source, _, _, part in pieces]),
        (held_bout_ref, bin_ref, *[target.at[part] for _, target, _, part in pieces]),
        sems,
    )
    for copy in copies[:2]:
        copy.wait()
    rows_ref[...] = held_ref[...].reshape(tokens * images, width)
    own = lax.axis_index(axis)
    for index in range(bout_ref.shape[1] // width):
        bias = jnp.where(own == index, held_bout_ref[...].astype(f32), 0.0)
        bout_ref[:, index * width : (index + 1) * width] = bias
    for copy, (_, target, turned, part) in zip(copies[2:], pieces):
        copy.wait()
        turned[:, part] = target[part].T


def steps(size, first):
    return [1] + list(range(size - 1, 1, -1)) if first else list(range(size - 1, 0, -1))


def tree_sum(refs, first):
    order = [0] + steps(len(refs), first)
    values = [refs[order.index(step)][...].astype(f32) for step in range(len(refs))]
    while len(values) > 1:
        values = [values[k] + values[k + 1] for k in range(0, len(values), 2)]
    return values[0]


def dispatch_kernel(images, count, *refs):
    parts, (rows_ref, grads_ref, sent_ref, dispatch_ref, combine_ref, total_ref) = refs[:count], refs[count:]
    logits = tree_sum(parts, True)
    top = jnp.max(logits, axis=0, keepdims=True)
    powers = jnp.exp(logits - top)
    sums = jnp.sum(powers, axis=0, keepdims=True)
    combine = powers / sums
    total_ref[...] = top + jnp.log(sums)
    powers = jnp.exp(logits - by_image(logits, images, jnp.max, -jnp.inf))
    dispatch = powers / by_image(powers, images, jnp.sum, 0.0)
    combine_ref[...] = combine
    dispatch_ref[...] = dispatch
    send(sent_ref, [dot(spread(dispatch, images), rows_ref[...], 1, 0)], [dot(spread(combine, images), grads_ref[...], 1, 0)])


def send(sent_ref, forward, backward):
    groups, hidden, images, width = sent_ref.shape
    width //= 2
    for half, parts in enumerate((forward, backward)):
        parts = [part.astype(bf16).reshape(groups, images, width) for part in parts]
        for index in range(hidden):
            sent_ref[:, index, :, half * width : (half + 1) * width] = parts[index % len(parts)]


def expert_kernel(came_ref, bout_ref, bin_ref, wout_ref, win_ref, wout_turned_ref, win_turned_ref, sent_ref):
    groups, hidden, images, width = came_ref.shape
    came = [came_ref[:, index].reshape(groups * images, width) for index in range(hidden)]
    width //= 2
    forward = jnp.concatenate([part[:, :width] for part in came], axis=1)
    backward = jnp.concatenate([part[:, width:] for part in came], axis=1)
    activated, slope = gelu_parts(dot(forward, win_ref[...], 1, 0) + bin_ref[...].astype(f32))
    hidden_grad = dot(backward, wout_turned_ref[...], 1, 0)
    out = dot(activated.astype(bf16), wout_ref[...], 1, 0) + bout_ref[...]
    back = dot((hidden_grad * slope).astype(bf16), win_turned_ref[...], 1, 0)
    parts = [slice(index * width, (index + 1) * width) for index in range(hidden)]
    send(sent_ref, [out[:, part] for part in parts], [back[:, part] for part in parts])


def gradient_kernel(came_ref, rows_ref, grads_ref, dispatch_ref, combine_ref, out_ref, back_ref, part_ref):
    slots, hidden, images, width = came_ref.shape
    came = came_ref[:, 0].astype(f32)
    for index in range(1, hidden):
        came = came + came_ref[:, index].astype(f32)
    came = came.astype(bf16).reshape(slots * images, width)
    out, back = came[:, : width // 2], came[:, width // 2 :]
    out_ref[...], back_ref[...] = out, back
    combine_grad = gather(dot(out, grads_ref[...], 1, 1), images)
    dispatch_grad = gather(dot(back, rows_ref[...], 1, 1), images)
    combine, dispatch = combine_ref[...], dispatch_ref[...]
    part = combine * (combine_grad - jnp.sum(combine * combine_grad, axis=0, keepdims=True))
    part = part + dispatch * (dispatch_grad - by_image(dispatch * dispatch_grad, images, jnp.sum, 0.0))
    part_ref[...] = part.astype(bf16)


def mixed_kernel(dispatch_ref, combine_ref, total_ref, out_ref, back_ref, mixed_ref, direct_ref, loss_ref):
    images = loss_ref.shape[0]
    mixed_ref[...] = dot(spread(combine_ref[...], images), out_ref[...], 0, 0).astype(bf16).reshape(mixed_ref.shape)
    direct_ref[...] = dot(spread(dispatch_ref[...], images), back_ref[...], 0, 0)
    total = jnp.broadcast_to(total_ref[...], (8, total_ref.shape[1]))
    tokens = loss_ref.shape[1]
    row, token = iota((images * tokens, tokens), 0), iota((images * tokens, tokens), 1)
    for index in range(images):
        pick = jnp.where(row == images * token + index, 1.0, 0.0)
        own = lax.dot_general(
            total, pick, (((1,), (0,)), ((), ())), precision=lax.Precision.HIGHEST, preferred_element_type=f32
        )[:1]
        loss_ref[index : index + 1] = loss_weight * own * own


def token_kernel(count, *refs):
    parts, refs = refs[:count], refs[count:]
    (combine_ref, total_ref, keys_ref, direct_ref, mixed_ref, loss_ref) = refs[:6]
    (out_ref, mixed_out_ref, loss_out_ref, held_ref, sems) = refs[6:]
    copies = load((mixed_ref, loss_ref), (mixed_out_ref, loss_out_ref), sems)
    logit_grad = tree_sum(parts, False) + 2.0 * loss_weight * total_ref[...] * combine_ref[...]
    out = dot(logit_grad.astype(bf16), keys_ref[...], 0, 0) + direct_ref[...]
    held_ref[...] = out.astype(bf16).reshape(held_ref.shape)
    last = pltpu.make_async_copy(held_ref, out_ref, sems.at[2])
    last.start()
    for copy in (*copies, last):
        copy.wait()


def call(kernel, outs, args, name, limit=8, far=(), far_outs=False, scratch=(), cost=None):
    return pl.pallas_call(
        kernel,
        out_shape=outs,
        in_specs=[VMEM] * len(args) + [HBM] * len(far),
        out_specs=[HBM if far_outs else VMEM] * len(outs),
        scratch_shapes=scratch,
        compiler_params=pltpu.CompilerParams(vmem_limit_bytes=limit * MIB),
        cost_estimate=cost,
        name=name,
    )(*args, *(pltpu.with_memory_space_constraint(value, pltpu.HBM) for value in far))


def exchange(value, axis, first):
    size = lax.axis_size(axis)
    return [value] + [
        lax.ppermute(value, axis, [(source, source ^ step) for source in range(size)]) for step in steps(size, first)
    ]


def per_device(tokens, slot_params, weight_in, bias_in, weight_out, bias_out, cotangent):
    images, count, width = tokens.shape
    groups, hidden = lax.axis_size(expert), lax.axis_size("hidden")
    slots = slot_params.shape[1]
    wide = weight_in.shape[1]
    rows = images * count
    weight_in, weight_out = weight_in[0], weight_out[0]
    by_token = jnp.transpose(tokens, (1, 0, 2))
    grad_by_token = jnp.transpose(cotangent, (1, 0, 2))
    table = pltpu.VMEM((slots, rows), f32)
    row_shape = pltpu.VMEM((rows, width), bf16)
    held_shape = pltpu.VMEM(by_token.shape, bf16)
    sent_shape = pltpu.VMEM((groups, hidden, images, 2 * width), bf16)

    part, token_rows, keys, raw = call(
        lambda *refs: logits_kernel(lax.axis_size("expert_c"), *refs),
        [table, row_shape, pltpu.VMEM((slots, width), bf16), held_shape],
        (),
        "logits",
        far=(by_token, jnp.transpose(slot_params), grad_by_token),
        scratch=[held_shape, pltpu.VMEM((slots, width), bf16), pltpu.SemaphoreType.DMA((3,))],
    )
    grad_rows, *expert_values = call(
        lambda *refs: prepare_kernel("hidden", *refs),
        [
            row_shape,
            pltpu.VMEM((1, wide), f32),
            *[pltpu.VMEM(value.shape, bf16) for value in (bias_in, weight_out, weight_in)],
            *[pltpu.VMEM(value.shape[::-1], bf16) for value in (weight_out, weight_in)],
        ],
        (raw,),
        "prepare",
        far=(bias_out, bias_in, weight_out, weight_in),
        scratch=[
            pltpu.VMEM(bias_out.shape, bf16),
            pltpu.SemaphoreType.DMA((2 + 2 * weight_pieces,)),
        ],
    )
    parts = exchange(part, "hidden", True)
    sent, dispatch, combine, total = call(
        lambda *refs: dispatch_kernel(images, hidden, *refs),
        [sent_shape, table, table, pltpu.VMEM((1, rows), f32)],
        (*parts, token_rows, grad_rows),
        "dispatch",
    )

    def to_all(value):
        value = value.reshape(groups * hidden, images, 2 * width)
        value = lax.all_to_all(value, send_order, split_axis=0, concat_axis=0, tiled=True)
        return value.reshape(groups, hidden, images, 2 * width)

    (sent,) = call(
        expert_kernel,
        [sent_shape],
        (to_all(sent), *expert_values),
        "expert",
        24,
    )
    slot_out, in_grad, part = call(
        gradient_kernel,
        [*[pltpu.VMEM((slots * images, width), bf16)] * 2, pltpu.VMEM((slots, rows), bf16)],
        (to_all(sent), token_rows, grad_rows, dispatch, combine),
        "gradient",
    )
    parts = exchange(part, "hidden", False)
    mixed, direct, zloss = call(
        mixed_kernel,
        [held_shape, pltpu.VMEM((rows, width), f32), pltpu.VMEM((images, count), f32)],
        (dispatch, combine, total, slot_out, in_grad),
        "mixed",
    )
    out_shape = jax.ShapeDtypeStruct(by_token.shape, bf16)
    token_grad, mixed, zloss = call(
        lambda *refs: token_kernel(hidden, *refs),
        [out_shape, out_shape, jax.ShapeDtypeStruct((images, count), f32)],
        (*parts, combine, total, keys, direct, mixed, zloss),
        "token_grad",
        far_outs=True,
        scratch=[held_shape, pltpu.SemaphoreType.DMA((3,))],
    )
    return (jnp.transpose(mixed, (1, 0, 2)), jnp.transpose(token_grad, (1, 0, 2)), zloss)


def solution(mesh):
    groups, hidden = mesh.devices.shape
    halves = 2 if groups % 4 == 0 else 1
    parts = (halves, groups // (halves * halves), halves, hidden)
    return jax.shard_map(
        per_device,
        mesh=jax.sharding.Mesh(mesh.devices.reshape(parts), (*expert, "hidden")),
        in_specs=(
            P(expert, None, "hidden"),
            P("hidden", None),
            P(expert, None, "hidden"),
            P(expert, "hidden"),
            P(expert, "hidden", None),
            P(expert, "hidden"),
            P(expert, None, "hidden"),
        ),
        out_specs=(P(expert, None, "hidden"), P(expert, None, "hidden"), P(expert, None)),
        check_vma=False,
    )
```

```python
import jax
import jax.numpy as jnp
from jax import lax
from jax.experimental import pallas as pl
from jax.experimental.pallas import tpu as pltpu
from jax.sharding import PartitionSpec as P

loss_weight = 0.1
f32, bf16 = jnp.float32, jnp.bfloat16
VMEM = pl.BlockSpec(memory_space=pltpu.VMEM)
HBM = pl.BlockSpec(memory_space=pltpu.HBM)
MIB = 1024 * 1024
expert = ("expert_a", "expert_b", "expert_c")
send_order = ("expert_a", "expert_c", "expert_b", "hidden")
weight_pieces = 2


def gelu_parts(value):
    factor = 0.7978845608028654
    inner = factor * (value + 0.044715 * value * value * value)
    slope_tanh = jnp.tanh(inner)
    result = 0.5 * value * (1.0 + slope_tanh)
    slope = 0.5 * (1.0 + slope_tanh) + 0.5 * value * (1.0 - slope_tanh * slope_tanh) * factor * (
        1.0 + 3.0 * 0.044715 * value * value
    )
    return (result, slope)


def dot(lhs, rhs, lhs_dim, rhs_dim):
    dims = (((lhs_dim,), (rhs_dim,)), ((), ()))
    return lax.dot_general(lhs, rhs, dims, preferred_element_type=f32)


def modulo(value, size):
    return value & (size - 1) if size & (size - 1) == 0 else lax.rem(value, size)


def iota(shape, dim):
    return lax.broadcasted_iota(jnp.int32, shape, dim)


def same_image(rows, tokens, images):
    return modulo(iota((rows, tokens), 0), images) == modulo(iota((rows, tokens), 1), images)


def spread(values, images):
    slots, tokens = values.shape
    first = images * iota((images * slots, slots), 1)
    row = iota((images * slots, slots), 0)
    pick = jnp.where((row >= first) & (row < first + images), 1.0, 0.0).astype(bf16)
    wide = dot(pick, values.astype(bf16), 1, 0)
    return jnp.where(same_image(images * slots, tokens, images), wide, 0.0).astype(bf16)


def gather(values, images):
    rows, tokens = values.shape
    values = jnp.where(same_image(rows, tokens, images), values, 0.0)
    return jnp.sum(values.reshape(rows // images, images, tokens), axis=1)


def by_image(values, images, reduce, fill):
    image = modulo(iota(values.shape, 1), images)
    result = None
    for index in range(images):
        here = image == index
        part = reduce(jnp.where(here, values, fill), axis=1, keepdims=True)
        result = part if result is None else jnp.where(here, part, result)
    return jnp.broadcast_to(result, values.shape)


def load(sources, targets, sems):
    copies = [pltpu.make_async_copy(*pair, sems.at[k]) for k, pair in enumerate(zip(sources, targets))]
    for copy in copies:
        copy.start()
    return copies


def in_turn(keys, halves):
    slots = keys.shape[0]
    middle = slots // (halves * halves)
    to, source = iota((slots, slots), 0), iota((slots, slots), 1)
    pick = jnp.zeros((slots, slots), f32)
    for a in range(halves):
        for c in range(halves):
            b = to - (a * halves + c) * middle
            here = (b >= 0) & (b < middle) & (source == (a * middle + b) * halves + c)
            pick = jnp.where(here, 1.0, pick)
    return dot(pick.astype(bf16), keys, 1, 0).astype(bf16)


def logits_kernel(halves, tokens_ref, keys_in_ref, part_ref, rows_ref, keys_ref, held_ref, held_keys_ref, sems):
    tokens, images, width = tokens_ref.shape
    copies = load((tokens_ref, keys_in_ref), (held_ref, held_keys_ref), sems)
    copies[1].wait()
    keys_ref[...] = in_turn(held_keys_ref[...], halves)
    copies[0].wait()
    rows = held_ref[...].reshape(tokens * images, width)
    rows_ref[...] = rows
    part_ref[...] = dot(keys_ref[...], rows, 1, 1)


def prepare_kernel(axis, after_ref, tokens_ref, bout_in_ref, bin_in_ref, wout_in_ref, win_in_ref,
                   rows_ref, bout_ref, bin_ref, wout_ref, win_ref, wout_turned_ref, win_turned_ref,
                   held_ref, held_bout_ref, sems):
    del after_ref
    tokens, images, width = tokens_ref.shape
    pieces = []
    for source, target, turned in (
        (wout_in_ref, wout_ref, wout_turned_ref), (win_in_ref, win_ref, win_turned_ref)
    ):
        step = source.shape[0] // weight_pieces
        pieces += [(source, target, turned, pl.ds(k * step, step)) for k in range(weight_pieces)]
    copies = load(
        (tokens_ref, bout_in_ref, bin_in_ref, *[source.at[part] for source, _, _, part in pieces]),
        (held_ref, held_bout_ref, bin_ref, *[target.at[part] for _, target, _, part in pieces]),
        sems,
    )
    for copy in copies[:3]:
        copy.wait()
    rows_ref[...] = held_ref[...].reshape(tokens * images, width)
    own = lax.axis_index(axis)
    for index in range(bout_ref.shape[1] // width):
        bias = jnp.where(own == index, held_bout_ref[...].astype(f32), 0.0)
        bout_ref[:, index * width : (index + 1) * width] = bias
    for copy, (_, target, turned, part) in zip(copies[3:], pieces):
        copy.wait()
        turned[:, part] = target[part].T


def steps(size, first):
    return list(range(2, size)) + [1] if first else list(range(1, size))


def tree_sum(refs, first):
    order = [0] + steps(len(refs), first)
    values = [refs[order.index(step)][...].astype(f32) for step in range(len(refs))]
    while len(values) > 1:
        values = [values[k] + values[k + 1] for k in range(0, len(values), 2)]
    return values[0]


def dispatch_kernel(images, count, *refs):
    parts, (rows_ref, grads_ref, sent_ref, dispatch_ref, combine_ref, norm_ref) = refs[:count], refs[count:]
    logits = tree_sum(parts, True)
    top = jnp.max(logits, axis=0, keepdims=True)
    powers = jnp.exp(logits - top)
    sums = jnp.sum(powers, axis=0, keepdims=True)
    combine = powers / sums
    norm_ref[0:1], norm_ref[1:2] = top, sums
    powers = jnp.exp(logits - by_image(logits, images, jnp.max, -jnp.inf))
    dispatch = powers / by_image(powers, images, jnp.sum, 0.0)
    combine_ref[...] = combine
    dispatch_ref[...] = dispatch
    send(sent_ref, [dot(spread(dispatch, images), rows_ref[...], 1, 0)], [dot(spread(combine, images), grads_ref[...], 1, 0)])


def send(sent_ref, forward, backward):
    groups, hidden, images, width = sent_ref.shape
    width //= 2
    for half, parts in enumerate((forward, backward)):
        parts = [part.astype(bf16).reshape(groups, images, width) for part in parts]
        for index in range(hidden):
            sent_ref[:, index, :, half * width : (half + 1) * width] = parts[index % len(parts)]


def expert_kernel(came_ref, bout_ref, bin_ref, wout_ref, win_ref, wout_turned_ref, win_turned_ref, sent_ref):
    groups, hidden, images, width = came_ref.shape
    came = [came_ref[:, index].reshape(groups * images, width) for index in range(hidden)]
    width //= 2
    forward = jnp.concatenate([part[:, :width] for part in came], axis=1)
    backward = jnp.concatenate([part[:, width:] for part in came], axis=1)
    activated, slope = gelu_parts(dot(forward, win_ref[...], 1, 0) + bin_ref[...].astype(f32))
    hidden_grad = dot(backward, wout_turned_ref[...], 1, 0)
    out = dot(activated.astype(bf16), wout_ref[...], 1, 0) + bout_ref[...]
    back = dot((hidden_grad * slope).astype(bf16), win_turned_ref[...], 1, 0)
    parts = [slice(index * width, (index + 1) * width) for index in range(hidden)]
    send(sent_ref, [out[:, part] for part in parts], [back[:, part] for part in parts])


def gradient_kernel(came_ref, rows_ref, grads_ref, dispatch_ref, combine_ref, out_ref, back_ref, part_ref):
    slots, hidden, images, width = came_ref.shape
    came = came_ref[:, 0].astype(f32)
    for index in range(1, hidden):
        came = came + came_ref[:, index].astype(f32)
    came = came.astype(bf16).reshape(slots * images, width)
    out, back = came[:, : width // 2], came[:, width // 2 :]
    out_ref[...], back_ref[...] = out, back
    combine_grad = gather(dot(out, grads_ref[...], 1, 1), images)
    dispatch_grad = gather(dot(back, rows_ref[...], 1, 1), images)
    combine, dispatch = combine_ref[...], dispatch_ref[...]
    part = combine * (combine_grad - jnp.sum(combine * combine_grad, axis=0, keepdims=True))
    part = part + dispatch * (dispatch_grad - by_image(dispatch * dispatch_grad, images, jnp.sum, 0.0))
    part_ref[...] = part.astype(bf16)


def mixed_kernel(dispatch_ref, combine_ref, norm_ref, keys_ref, out_ref, back_ref,
                 mixed_out_ref, loss_out_ref, direct_ref, mixed_ref, loss_ref, sems):
    images = loss_ref.shape[0]
    mixed_ref[...] = dot(spread(combine_ref[...], images), out_ref[...], 0, 0).astype(bf16).reshape(mixed_ref.shape)
    copies = load((mixed_ref,), (mixed_out_ref,), sems)
    total = norm_ref[0:1] + jnp.log(norm_ref[1:2])
    known = 2.0 * loss_weight * total * combine_ref[...]
    direct = dot(spread(dispatch_ref[...], images), back_ref[...], 0, 0)
    direct_ref[...] = direct + dot(known.astype(bf16), keys_ref[...], 0, 0)
    total = jnp.broadcast_to(total, (8, total.shape[1]))
    tokens = loss_ref.shape[1]
    row, token = iota((images * tokens, tokens), 0), iota((images * tokens, tokens), 1)
    for index in range(images):
        pick = jnp.where(row == images * token + index, 1.0, 0.0)
        own = lax.dot_general(
            total, pick, (((1,), (0,)), ((), ())), precision=lax.Precision.HIGHEST, preferred_element_type=f32
        )[:1]
        loss_ref[index : index + 1] = loss_weight * own * own
    last = pltpu.make_async_copy(loss_ref, loss_out_ref, sems.at[1])
    last.start()
    for copy in (*copies, last):
        copy.wait()


def token_kernel(count, *refs):
    parts, refs = refs[:count], refs[count:]
    keys_ref, direct_ref, out_ref, held_ref, sem = refs
    logit_grad = tree_sum(parts, False)
    out = dot(logit_grad.astype(bf16), keys_ref[...], 0, 0) + direct_ref[...]
    held_ref[...] = out.astype(bf16).reshape(held_ref.shape)
    copy = pltpu.make_async_copy(held_ref, out_ref, sem)
    copy.start()
    copy.wait()


def call(kernel, outs, args, name, limit=8, far=(), far_outs=0, scratch=(), cost=None):
    return pl.pallas_call(
        kernel,
        out_shape=outs,
        in_specs=[VMEM] * len(args) + [HBM] * len(far),
        out_specs=[HBM] * far_outs + [VMEM] * (len(outs) - far_outs),
        scratch_shapes=scratch,
        compiler_params=pltpu.CompilerParams(vmem_limit_bytes=limit * MIB),
        cost_estimate=cost,
        name=name,
    )(*args, *(pltpu.with_memory_space_constraint(value, pltpu.HBM) for value in far))


def exchange(value, axis, first):
    size = lax.axis_size(axis)
    return [value] + [
        lax.ppermute(value, axis, [(source, source ^ step) for source in range(size)]) for step in steps(size, first)
    ]


def per_device(tokens, slot_params, weight_in, bias_in, weight_out, bias_out, cotangent):
    images, count, width = tokens.shape
    groups, hidden = lax.axis_size(expert), lax.axis_size("hidden")
    slots = slot_params.shape[1]
    wide = weight_in.shape[1]
    rows = images * count
    weight_in, weight_out = weight_in[0], weight_out[0]
    by_token = jnp.transpose(tokens, (1, 0, 2))
    grad_by_token = jnp.transpose(cotangent, (1, 0, 2))
    table = pltpu.VMEM((slots, rows), f32)
    row_shape = pltpu.VMEM((rows, width), bf16)
    held_shape = pltpu.VMEM(by_token.shape, bf16)
    sent_shape = pltpu.VMEM((groups, hidden, images, 2 * width), bf16)

    part, token_rows, keys = call(
        lambda *refs: logits_kernel(lax.axis_size("expert_c"), *refs),
        [table, row_shape, pltpu.VMEM((slots, width), bf16)],
        (),
        "logits",
        far=(by_token, jnp.transpose(slot_params)),
        scratch=[held_shape, pltpu.VMEM((slots, width), bf16), pltpu.SemaphoreType.DMA((2,))],
    )
    grad_rows, *expert_values = call(
        lambda *refs: prepare_kernel("hidden", *refs),
        [
            row_shape,
            pltpu.VMEM((1, wide), f32),
            *[pltpu.VMEM(value.shape, bf16) for value in (bias_in, weight_out, weight_in)],
            *[pltpu.VMEM(value.shape[::-1], bf16) for value in (weight_out, weight_in)],
        ],
        (part,),
        "prepare",
        far=(grad_by_token, bias_out, bias_in, weight_out, weight_in),
        scratch=[
            held_shape,
            pltpu.VMEM(bias_out.shape, bf16),
            pltpu.SemaphoreType.DMA((3 + 2 * weight_pieces,)),
        ],
    )
    parts = exchange(part, "hidden", True)
    sent, dispatch, combine, total = call(
        lambda *refs: dispatch_kernel(images, hidden, *refs),
        [sent_shape, table, table, pltpu.VMEM((2, rows), f32)],
        (*parts, token_rows, grad_rows),
        "dispatch",
    )

    def to_all(value):
        value = value.reshape(groups * hidden, images, 2 * width)
        value = lax.all_to_all(value, send_order, split_axis=0, concat_axis=0, tiled=True)
        return value.reshape(groups, hidden, images, 2 * width)

    (sent,) = call(
        expert_kernel,
        [sent_shape],
        (to_all(sent), *expert_values),
        "expert",
        24,
    )
    slot_out, in_grad, part = call(
        gradient_kernel,
        [*[pltpu.VMEM((slots * images, width), bf16)] * 2, pltpu.VMEM((slots, rows), bf16)],
        (to_all(sent), token_rows, grad_rows, dispatch, combine),
        "gradient",
    )
    parts = exchange(part, "hidden", False)
    out_shape, loss_shape = jax.ShapeDtypeStruct(by_token.shape, bf16), (images, count)
    mixed, zloss, direct = call(
        mixed_kernel,
        [out_shape, jax.ShapeDtypeStruct(loss_shape, f32), pltpu.VMEM((rows, width), f32)],
        (dispatch, combine, total, keys, slot_out, in_grad),
        "mixed",
        far_outs=2,
        scratch=[held_shape, pltpu.VMEM(loss_shape, f32), pltpu.SemaphoreType.DMA((2,))],
    )
    (token_grad,) = call(
        lambda *refs: token_kernel(hidden, *refs),
        [out_shape],
        (*parts, keys, direct),
        "token_grad",
        far_outs=1,
        scratch=[held_shape, pltpu.SemaphoreType.DMA],
    )
    return (jnp.transpose(mixed, (1, 0, 2)), jnp.transpose(token_grad, (1, 0, 2)), zloss)


def solution(mesh):
    groups, hidden = mesh.devices.shape
    halves = 2 if groups % 4 == 0 else 1
    parts = (halves, groups // (halves * halves), halves, hidden)
    return jax.shard_map(
        per_device,
        mesh=jax.sharding.Mesh(mesh.devices.reshape(parts), (*expert, "hidden")),
        in_specs=(
            P(expert, None, "hidden"),
            P("hidden", None),
            P(expert, None, "hidden"),
            P(expert, "hidden"),
            P(expert, "hidden", None),
            P(expert, "hidden"),
            P(expert, None, "hidden"),
        ),
        out_specs=(P(expert, None, "hidden"), P(expert, None, "hidden"), P(expert, None)),
        check_vma=False,
    )
```

```python
import jax
import jax.numpy as jnp
from jax import lax
from jax.experimental import pallas as pl
from jax.experimental.pallas import tpu as pltpu
from jax.sharding import PartitionSpec as P

loss_weight = 0.1
f32, bf16 = jnp.float32, jnp.bfloat16
VMEM = pl.BlockSpec(memory_space=pltpu.VMEM)
HBM = pl.BlockSpec(memory_space=pltpu.HBM)
MIB = 1024 * 1024
expert = ("expert_a", "expert_b", "expert_c")
send_order = ("expert_a", "expert_c", "expert_b", "hidden")
weight_pieces = 4


def gelu_parts(value):
    factor = 0.7978845608028654
    inner = factor * (value + 0.044715 * value * value * value)
    slope_tanh = jnp.tanh(inner)
    result = 0.5 * value * (1.0 + slope_tanh)
    slope = 0.5 * (1.0 + slope_tanh) + 0.5 * value * (1.0 - slope_tanh * slope_tanh) * factor * (
        1.0 + 3.0 * 0.044715 * value * value
    )
    return (result, slope)


def dot(lhs, rhs, lhs_dim, rhs_dim):
    dims = (((lhs_dim,), (rhs_dim,)), ((), ()))
    return lax.dot_general(lhs, rhs, dims, preferred_element_type=f32)


def modulo(value, size):
    return value & (size - 1) if size & (size - 1) == 0 else lax.rem(value, size)


def iota(shape, dim):
    return lax.broadcasted_iota(jnp.int32, shape, dim)


def same_image(rows, tokens, images):
    return modulo(iota((rows, tokens), 0), images) == modulo(iota((rows, tokens), 1), images)


def spread(values, images):
    slots, tokens = values.shape
    first = images * iota((images * slots, slots), 1)
    row = iota((images * slots, slots), 0)
    pick = jnp.where((row >= first) & (row < first + images), 1.0, 0.0).astype(bf16)
    wide = dot(pick, values.astype(bf16), 1, 0)
    return jnp.where(same_image(images * slots, tokens, images), wide, 0.0).astype(bf16)


def gather(values, images):
    rows, tokens = values.shape
    values = jnp.where(same_image(rows, tokens, images), values, 0.0)
    return jnp.sum(values.reshape(rows // images, images, tokens), axis=1)


def by_image(values, images, reduce, fill):
    image = modulo(iota(values.shape, 1), images)
    result = None
    for index in range(images):
        here = image == index
        part = reduce(jnp.where(here, values, fill), axis=1, keepdims=True)
        result = part if result is None else jnp.where(here, part, result)
    return jnp.broadcast_to(result, values.shape)


def load(sources, targets, sems):
    copies = [pltpu.make_async_copy(*pair, sems.at[k]) for k, pair in enumerate(zip(sources, targets))]
    for copy in copies:
        copy.start()
    return copies


def in_turn(keys, halves):
    slots = keys.shape[0]
    middle = slots // (halves * halves)
    to, source = iota((slots, slots), 0), iota((slots, slots), 1)
    pick = jnp.zeros((slots, slots), f32)
    for a in range(halves):
        for c in range(halves):
            b = to - (a * halves + c) * middle
            here = (b >= 0) & (b < middle) & (source == (a * middle + b) * halves + c)
            pick = jnp.where(here, 1.0, pick)
    return dot(pick.astype(bf16), keys, 1, 0).astype(bf16)


def logits_kernel(halves, tokens_ref, keys_in_ref, part_ref, rows_ref, keys_ref, held_ref, held_keys_ref, sems):
    tokens, images, width = tokens_ref.shape
    copies = load((tokens_ref, keys_in_ref), (held_ref, held_keys_ref), sems)
    copies[1].wait()
    keys_ref[...] = in_turn(held_keys_ref[...], halves)
    copies[0].wait()
    rows = held_ref[...].reshape(tokens * images, width)
    rows_ref[...] = rows
    part_ref[...] = dot(keys_ref[...], rows, 1, 1)


def prepare_kernel(axis, after_ref, tokens_ref, bout_in_ref, bin_in_ref, wout_in_ref, win_in_ref,
                   rows_ref, bout_ref, bin_ref, wout_ref, win_ref, wout_turned_ref, win_turned_ref,
                   held_ref, held_bout_ref, sems):
    del after_ref
    tokens, images, width = tokens_ref.shape
    pieces = []
    for source, target, turned in (
        (wout_in_ref, wout_ref, wout_turned_ref), (win_in_ref, win_ref, win_turned_ref)
    ):
        step = source.shape[0] // weight_pieces
        pieces += [(source, target, turned, pl.ds(k * step, step)) for k in range(weight_pieces)]
    copies = load(
        (tokens_ref, bout_in_ref, bin_in_ref, *[source.at[part] for source, _, _, part in pieces]),
        (held_ref, held_bout_ref, bin_ref, *[target.at[part] for _, target, _, part in pieces]),
        sems,
    )
    for copy in copies[:3]:
        copy.wait()
    rows_ref[...] = held_ref[...].reshape(tokens * images, width)
    own = lax.axis_index(axis)
    for index in range(bout_ref.shape[1] // width):
        bias = jnp.where(own == index, held_bout_ref[...].astype(f32), 0.0)
        bout_ref[:, index * width : (index + 1) * width] = bias
    for copy, (_, target, turned, part) in zip(copies[3:], pieces):
        copy.wait()
        turned[:, part] = target[part].T


def steps(size, first):
    return list(range(2, size)) + [1] if first else list(range(1, size))


def tree_sum(refs, first):
    order = [0] + steps(len(refs), first)
    values = [refs[order.index(step)][...].astype(f32) for step in range(len(refs))]
    while len(values) > 1:
        values = [values[k] + values[k + 1] for k in range(0, len(values), 2)]
    return values[0]


def dispatch_kernel(images, count, *refs):
    parts, (rows_ref, grads_ref, sent_ref, dispatch_ref, combine_ref, total_ref) = refs[:count], refs[count:]
    logits = tree_sum(parts, True)
    top = jnp.max(logits, axis=0, keepdims=True)
    powers = jnp.exp(logits - top)
    sums = jnp.sum(powers, axis=0, keepdims=True)
    combine = powers / sums
    total_ref[...] = top + jnp.log(sums)
    powers = jnp.exp(logits - by_image(logits, images, jnp.max, -jnp.inf))
    dispatch = powers / by_image(powers, images, jnp.sum, 0.0)
    combine_ref[...] = combine
    dispatch_ref[...] = dispatch
    send(sent_ref, [dot(spread(dispatch, images), rows_ref[...], 1, 0)], [dot(spread(combine, images), grads_ref[...], 1, 0)])


def send(sent_ref, forward, backward):
    groups, hidden, images, width = sent_ref.shape
    width //= 2
    for half, parts in enumerate((forward, backward)):
        parts = [part.astype(bf16).reshape(groups, images, width) for part in parts]
        for index in range(hidden):
            sent_ref[:, index, :, half * width : (half + 1) * width] = parts[index % len(parts)]


def expert_kernel(came_ref, bout_ref, bin_ref, wout_ref, win_ref, wout_turned_ref, win_turned_ref, sent_ref):
    groups, hidden, images, width = came_ref.shape
    came = [came_ref[:, index].reshape(groups * images, width) for index in range(hidden)]
    width //= 2
    forward = jnp.concatenate([part[:, :width] for part in came], axis=1)
    backward = jnp.concatenate([part[:, width:] for part in came], axis=1)
    activated, slope = gelu_parts(dot(forward, win_ref[...], 1, 0) + bin_ref[...].astype(f32))
    hidden_grad = dot(backward, wout_turned_ref[...], 1, 0)
    out = dot(activated.astype(bf16), wout_ref[...], 1, 0) + bout_ref[...]
    back = dot((hidden_grad * slope).astype(bf16), win_turned_ref[...], 1, 0)
    parts = [slice(index * width, (index + 1) * width) for index in range(hidden)]
    send(sent_ref, [out[:, part] for part in parts], [back[:, part] for part in parts])


def gradient_kernel(came_ref, rows_ref, grads_ref, dispatch_ref, combine_ref, out_ref, back_ref, part_ref):
    slots, hidden, images, width = came_ref.shape
    came = came_ref[:, 0].astype(f32)
    for index in range(1, hidden):
        came = came + came_ref[:, index].astype(f32)
    came = came.astype(bf16).reshape(slots * images, width)
    out, back = came[:, : width // 2], came[:, width // 2 :]
    out_ref[...], back_ref[...] = out, back
    combine_grad = gather(dot(out, grads_ref[...], 1, 1), images)
    dispatch_grad = gather(dot(back, rows_ref[...], 1, 1), images)
    combine, dispatch = combine_ref[...], dispatch_ref[...]
    part = combine * (combine_grad - jnp.sum(combine * combine_grad, axis=0, keepdims=True))
    part = part + dispatch * (dispatch_grad - by_image(dispatch * dispatch_grad, images, jnp.sum, 0.0))
    part_ref[...] = part.astype(bf16)


def mixed_kernel(dispatch_ref, combine_ref, total_ref, out_ref, back_ref, mixed_ref, direct_ref, loss_ref):
    images = loss_ref.shape[0]
    mixed_ref[...] = dot(spread(combine_ref[...], images), out_ref[...], 0, 0).astype(bf16).reshape(mixed_ref.shape)
    direct_ref[...] = dot(spread(dispatch_ref[...], images), back_ref[...], 0, 0)
    total = jnp.broadcast_to(total_ref[...], (8, total_ref.shape[1]))
    tokens = loss_ref.shape[1]
    row, token = iota((images * tokens, tokens), 0), iota((images * tokens, tokens), 1)
    for index in range(images):
        pick = jnp.where(row == images * token + index, 1.0, 0.0)
        own = lax.dot_general(
            total, pick, (((1,), (0,)), ((), ())), precision=lax.Precision.HIGHEST, preferred_element_type=f32
        )[:1]
        loss_ref[index : index + 1] = loss_weight * own * own


def token_kernel(count, *refs):
    parts, refs = refs[:count], refs[count:]
    (combine_ref, total_ref, keys_ref, direct_ref, mixed_ref, loss_ref) = refs[:6]
    (out_ref, mixed_out_ref, loss_out_ref, held_ref, sems) = refs[6:]
    copies = load((mixed_ref, loss_ref), (mixed_out_ref, loss_out_ref), sems)
    logit_grad = tree_sum(parts, False) + 2.0 * loss_weight * total_ref[...] * combine_ref[...]
    out = dot(logit_grad.astype(bf16), keys_ref[...], 0, 0) + direct_ref[...]
    held_ref[...] = out.astype(bf16).reshape(held_ref.shape)
    last = pltpu.make_async_copy(held_ref, out_ref, sems.at[2])
    last.start()
    for copy in (*copies, last):
        copy.wait()


def call(kernel, outs, args, name, limit=8, far=(), far_outs=False, scratch=(), cost=None):
    return pl.pallas_call(
        kernel,
        out_shape=outs,
        in_specs=[VMEM] * len(args) + [HBM] * len(far),
        out_specs=[HBM if far_outs else VMEM] * len(outs),
        scratch_shapes=scratch,
        compiler_params=pltpu.CompilerParams(vmem_limit_bytes=limit * MIB),
        cost_estimate=cost,
        name=name,
    )(*args, *(pltpu.with_memory_space_constraint(value, pltpu.HBM) for value in far))


def exchange(value, axis, first):
    size = lax.axis_size(axis)
    return [value] + [
        lax.ppermute(value, axis, [(source, source ^ step) for source in range(size)]) for step in steps(size, first)
    ]


def per_device(tokens, slot_params, weight_in, bias_in, weight_out, bias_out, cotangent):
    images, count, width = tokens.shape
    groups, hidden = lax.axis_size(expert), lax.axis_size("hidden")
    slots = slot_params.shape[1]
    wide = weight_in.shape[1]
    rows = images * count
    weight_in, weight_out = weight_in[0], weight_out[0]
    by_token = jnp.transpose(tokens, (1, 0, 2))
    grad_by_token = jnp.transpose(cotangent, (1, 0, 2))
    table = pltpu.VMEM((slots, rows), f32)
    row_shape = pltpu.VMEM((rows, width), bf16)
    held_shape = pltpu.VMEM(by_token.shape, bf16)
    sent_shape = pltpu.VMEM((groups, hidden, images, 2 * width), bf16)

    part, token_rows, keys = call(
        lambda *refs: logits_kernel(lax.axis_size("expert_c"), *refs),
        [table, row_shape, pltpu.VMEM((slots, width), bf16)],
        (),
        "logits",
        far=(by_token, jnp.transpose(slot_params)),
        scratch=[held_shape, pltpu.VMEM((slots, width), bf16), pltpu.SemaphoreType.DMA((2,))],
    )
    grad_rows, *expert_values = call(
        lambda *refs: prepare_kernel("hidden", *refs),
        [
            row_shape,
            pltpu.VMEM((1, wide), f32),
            *[pltpu.VMEM(value.shape, bf16) for value in (bias_in, weight_out, weight_in)],
            *[pltpu.VMEM(value.shape[::-1], bf16) for value in (weight_out, weight_in)],
        ],
        (part,),
        "prepare",
        far=(grad_by_token, bias_out, bias_in, weight_out, weight_in),
        scratch=[
            held_shape,
            pltpu.VMEM(bias_out.shape, bf16),
            pltpu.SemaphoreType.DMA((3 + 2 * weight_pieces,)),
        ],
    )
    parts = exchange(part, "hidden", True)
    sent, dispatch, combine, total = call(
        lambda *refs: dispatch_kernel(images, hidden, *refs),
        [sent_shape, table, table, pltpu.VMEM((1, rows), f32)],
        (*parts, token_rows, grad_rows),
        "dispatch",
    )

    def to_all(value):
        value = value.reshape(groups * hidden, images, 2 * width)
        value = lax.all_to_all(value, send_order, split_axis=0, concat_axis=0, tiled=True)
        return value.reshape(groups, hidden, images, 2 * width)

    (sent,) = call(
        expert_kernel,
        [sent_shape],
        (to_all(sent), *expert_values),
        "expert",
        24,
    )
    slot_out, in_grad, part = call(
        gradient_kernel,
        [*[pltpu.VMEM((slots * images, width), bf16)] * 2, pltpu.VMEM((slots, rows), bf16)],
        (to_all(sent), token_rows, grad_rows, dispatch, combine),
        "gradient",
    )
    parts = exchange(part, "hidden", False)
    mixed, direct, zloss = call(
        mixed_kernel,
        [held_shape, pltpu.VMEM((rows, width), f32), pltpu.VMEM((images, count), f32)],
        (dispatch, combine, total, slot_out, in_grad),
        "mixed",
    )
    out_shape = jax.ShapeDtypeStruct(by_token.shape, bf16)
    token_grad, mixed, zloss = call(
        lambda *refs: token_kernel(hidden, *refs),
        [out_shape, out_shape, jax.ShapeDtypeStruct((images, count), f32)],
        (*parts, combine, total, keys, direct, mixed, zloss),
        "token_grad",
        far_outs=True,
        scratch=[held_shape, pltpu.SemaphoreType.DMA((3,))],
    )
    return (jnp.transpose(mixed, (1, 0, 2)), jnp.transpose(token_grad, (1, 0, 2)), zloss)


def solution(mesh):
    groups, hidden = mesh.devices.shape
    halves = 2 if groups % 4 == 0 else 1
    parts = (halves, groups // (halves * halves), halves, hidden)
    return jax.shard_map(
        per_device,
        mesh=jax.sharding.Mesh(mesh.devices.reshape(parts), (*expert, "hidden")),
        in_specs=(
            P(expert, None, "hidden"),
            P("hidden", None),
            P(expert, None, "hidden"),
            P(expert, "hidden"),
            P(expert, "hidden", None),
            P(expert, "hidden"),
            P(expert, None, "hidden"),
        ),
        out_specs=(P(expert, None, "hidden"), P(expert, None, "hidden"), P(expert, None)),
        check_vma=False,
    )
```

```python
import jax
import jax.numpy as jnp
from jax import lax
from jax.experimental import pallas as pl
from jax.experimental.pallas import tpu as pltpu
from jax.sharding import PartitionSpec as P

loss_weight = 0.1
f32, bf16 = jnp.float32, jnp.bfloat16
VMEM = pl.BlockSpec(memory_space=pltpu.VMEM)
HBM = pl.BlockSpec(memory_space=pltpu.HBM)
MIB = 1024 * 1024
expert = ("expert_a", "expert_b", "expert_c")
send_order = ("expert_a", "expert_c", "expert_b", "hidden")
weight_pieces = 2


def gelu_parts(value):
    factor = 0.7978845608028654
    inner = factor * (value + 0.044715 * value * value * value)
    slope_tanh = jnp.tanh(inner)
    result = 0.5 * value * (1.0 + slope_tanh)
    slope = 0.5 * (1.0 + slope_tanh) + 0.5 * value * (1.0 - slope_tanh * slope_tanh) * factor * (
        1.0 + 3.0 * 0.044715 * value * value
    )
    return (result, slope)


def dot(lhs, rhs, lhs_dim, rhs_dim):
    dims = (((lhs_dim,), (rhs_dim,)), ((), ()))
    return lax.dot_general(lhs, rhs, dims, preferred_element_type=f32)


def modulo(value, size):
    return value & (size - 1) if size & (size - 1) == 0 else lax.rem(value, size)


def iota(shape, dim):
    return lax.broadcasted_iota(jnp.int32, shape, dim)


def same_image(rows, tokens, images):
    return modulo(iota((rows, tokens), 0), images) == modulo(iota((rows, tokens), 1), images)


def spread(values, images):
    slots, tokens = values.shape
    first = images * iota((images * slots, slots), 1)
    row = iota((images * slots, slots), 0)
    pick = jnp.where((row >= first) & (row < first + images), 1.0, 0.0).astype(bf16)
    wide = dot(pick, values.astype(bf16), 1, 0)
    return jnp.where(same_image(images * slots, tokens, images), wide, 0.0).astype(bf16)


def gather(values, images):
    rows, tokens = values.shape
    values = jnp.where(same_image(rows, tokens, images), values, 0.0)
    return jnp.sum(values.reshape(rows // images, images, tokens), axis=1)


def by_image(values, images, reduce, fill):
    image = modulo(iota(values.shape, 1), images)
    result = None
    for index in range(images):
        here = image == index
        part = reduce(jnp.where(here, values, fill), axis=1, keepdims=True)
        result = part if result is None else jnp.where(here, part, result)
    return jnp.broadcast_to(result, values.shape)


def load(sources, targets, sems):
    copies = [pltpu.make_async_copy(*pair, sems.at[k]) for k, pair in enumerate(zip(sources, targets))]
    for copy in copies:
        copy.start()
    return copies


def in_turn(keys, halves):
    slots = keys.shape[0]
    middle = slots // (halves * halves)
    to, source = iota((slots, slots), 0), iota((slots, slots), 1)
    pick = jnp.zeros((slots, slots), f32)
    for a in range(halves):
        for c in range(halves):
            b = to - (a * halves + c) * middle
            here = (b >= 0) & (b < middle) & (source == (a * middle + b) * halves + c)
            pick = jnp.where(here, 1.0, pick)
    return dot(pick.astype(bf16), keys, 1, 0).astype(bf16)


def logits_kernel(halves, tokens_ref, keys_in_ref, part_ref, rows_ref, keys_ref, held_ref, held_keys_ref, sems):
    tokens, images, width = tokens_ref.shape
    copies = load((tokens_ref, keys_in_ref), (held_ref, held_keys_ref), sems)
    copies[1].wait()
    keys_ref[...] = in_turn(held_keys_ref[...], halves)
    copies[0].wait()
    rows = held_ref[...].reshape(tokens * images, width)
    rows_ref[...] = rows
    part_ref[...] = dot(keys_ref[...], rows, 1, 1)


def prepare_kernel(axis, after_ref, tokens_ref, bout_in_ref, bin_in_ref, wout_in_ref, win_in_ref,
                   rows_ref, bout_ref, bin_ref, wout_ref, win_ref, wout_turned_ref, win_turned_ref,
                   held_ref, held_bout_ref, sems):
    del after_ref
    tokens, images, width = tokens_ref.shape
    pieces = []
    for source, target, turned in (
        (wout_in_ref, wout_ref, wout_turned_ref), (win_in_ref, win_ref, win_turned_ref)
    ):
        step = source.shape[0] // weight_pieces
        pieces += [(source, target, turned, pl.ds(k * step, step)) for k in range(weight_pieces)]
    copies = load(
        (tokens_ref, bout_in_ref, bin_in_ref, *[source.at[part] for source, _, _, part in pieces]),
        (held_ref, held_bout_ref, bin_ref, *[target.at[part] for _, target, _, part in pieces]),
        sems,
    )
    for copy in copies[:3]:
        copy.wait()
    rows_ref[...] = held_ref[...].reshape(tokens * images, width)
    own = lax.axis_index(axis)
    for index in range(bout_ref.shape[1] // width):
        bias = jnp.where(own == index, held_bout_ref[...].astype(f32), 0.0)
        bout_ref[:, index * width : (index + 1) * width] = bias
    for copy, (_, target, turned, part) in zip(copies[3:], pieces):
        copy.wait()
        turned[:, part] = target[part].T


def steps(size, first):
    return list(range(2, size)) + [1] if first else list(range(2, size - 1)) + [1] + list(range(size - 1, size))


def tree_sum(refs, first):
    order = [0] + steps(len(refs), first)
    values = [refs[order.index(step)][...].astype(f32) for step in range(len(refs))]
    while len(values) > 1:
        values = [values[k] + values[k + 1] for k in range(0, len(values), 2)]
    return values[0]


def dispatch_kernel(images, count, *refs):
    parts, (rows_ref, grads_ref, sent_ref, dispatch_ref, combine_ref, total_ref) = refs[:count], refs[count:]
    logits = tree_sum(parts, True)
    top = jnp.max(logits, axis=0, keepdims=True)
    powers = jnp.exp(logits - top)
    sums = jnp.sum(powers, axis=0, keepdims=True)
    combine = powers / sums
    total_ref[...] = top + jnp.log(sums)
    powers = jnp.exp(logits - by_image(logits, images, jnp.max, -jnp.inf))
    dispatch = powers / by_image(powers, images, jnp.sum, 0.0)
    combine_ref[...] = combine
    dispatch_ref[...] = dispatch
    send(sent_ref, [dot(spread(dispatch, images), rows_ref[...], 1, 0)], [dot(spread(combine, images), grads_ref[...], 1, 0)])


def send(sent_ref, forward, backward):
    groups, hidden, images, width = sent_ref.shape
    width //= 2
    for half, parts in enumerate((forward, backward)):
        parts = [part.astype(bf16).reshape(groups, images, width) for part in parts]
        for index in range(hidden):
            sent_ref[:, index, :, half * width : (half + 1) * width] = parts[index % len(parts)]


def expert_kernel(came_ref, bout_ref, bin_ref, wout_ref, win_ref, wout_turned_ref, win_turned_ref, sent_ref):
    groups, hidden, images, width = came_ref.shape
    came = [came_ref[:, index].reshape(groups * images, width) for index in range(hidden)]
    width //= 2
    forward = jnp.concatenate([part[:, :width] for part in came], axis=1)
    backward = jnp.concatenate([part[:, width:] for part in came], axis=1)
    activated, slope = gelu_parts(dot(forward, win_ref[...], 1, 0) + bin_ref[...].astype(f32))
    hidden_grad = dot(backward, wout_turned_ref[...], 1, 0)
    out = dot(activated.astype(bf16), wout_ref[...], 1, 0) + bout_ref[...]
    back = dot((hidden_grad * slope).astype(bf16), win_turned_ref[...], 1, 0)
    parts = [slice(index * width, (index + 1) * width) for index in range(hidden)]
    send(sent_ref, [out[:, part] for part in parts], [back[:, part] for part in parts])


def gradient_kernel(came_ref, rows_ref, grads_ref, dispatch_ref, combine_ref, out_ref, back_ref, part_ref):
    slots, hidden, images, width = came_ref.shape
    came = came_ref[:, 0].astype(f32)
    for index in range(1, hidden):
        came = came + came_ref[:, index].astype(f32)
    came = came.astype(bf16).reshape(slots * images, width)
    out, back = came[:, : width // 2], came[:, width // 2 :]
    out_ref[...], back_ref[...] = out, back
    combine_grad = gather(dot(out, grads_ref[...], 1, 1), images)
    dispatch_grad = gather(dot(back, rows_ref[...], 1, 1), images)
    combine, dispatch = combine_ref[...], dispatch_ref[...]
    part = combine * (combine_grad - jnp.sum(combine * combine_grad, axis=0, keepdims=True))
    part = part + dispatch * (dispatch_grad - by_image(dispatch * dispatch_grad, images, jnp.sum, 0.0))
    part_ref[...] = part.astype(bf16)


def mixed_kernel(dispatch_ref, combine_ref, total_ref, out_ref, back_ref, mixed_ref, direct_ref, loss_ref):
    images = loss_ref.shape[0]
    mixed_ref[...] = dot(spread(combine_ref[...], images), out_ref[...], 0, 0).astype(bf16).reshape(mixed_ref.shape)
    direct_ref[...] = dot(spread(dispatch_ref[...], images), back_ref[...], 0, 0)
    total = jnp.broadcast_to(total_ref[...], (8, total_ref.shape[1]))
    tokens = loss_ref.shape[1]
    row, token = iota((images * tokens, tokens), 0), iota((images * tokens, tokens), 1)
    for index in range(images):
        pick = jnp.where(row == images * token + index, 1.0, 0.0)
        own = lax.dot_general(
            total, pick, (((1,), (0,)), ((), ())), precision=lax.Precision.HIGHEST, preferred_element_type=f32
        )[:1]
        loss_ref[index : index + 1] = loss_weight * own * own


def token_kernel(count, *refs):
    parts, refs = refs[:count], refs[count:]
    (combine_ref, total_ref, keys_ref, direct_ref, mixed_ref, loss_ref) = refs[:6]
    (out_ref, mixed_out_ref, loss_out_ref, held_ref, sems) = refs[6:]
    copies = load((mixed_ref, loss_ref), (mixed_out_ref, loss_out_ref), sems)
    logit_grad = tree_sum(parts, False) + 2.0 * loss_weight * total_ref[...] * combine_ref[...]
    out = dot(logit_grad.astype(bf16), keys_ref[...], 0, 0) + direct_ref[...]
    held_ref[...] = out.astype(bf16).reshape(held_ref.shape)
    last = pltpu.make_async_copy(held_ref, out_ref, sems.at[2])
    last.start()
    for copy in (*copies, last):
        copy.wait()


def call(kernel, outs, args, name, limit=8, far=(), far_outs=False, scratch=(), cost=None):
    return pl.pallas_call(
        kernel,
        out_shape=outs,
        in_specs=[VMEM] * len(args) + [HBM] * len(far),
        out_specs=[HBM if far_outs else VMEM] * len(outs),
        scratch_shapes=scratch,
        compiler_params=pltpu.CompilerParams(vmem_limit_bytes=limit * MIB),
        cost_estimate=cost,
        name=name,
    )(*args, *(pltpu.with_memory_space_constraint(value, pltpu.HBM) for value in far))


def exchange(value, axis, first):
    size = lax.axis_size(axis)
    return [value] + [
        lax.ppermute(value, axis, [(source, source ^ step) for source in range(size)]) for step in steps(size, first)
    ]


def per_device(tokens, slot_params, weight_in, bias_in, weight_out, bias_out, cotangent):
    images, count, width = tokens.shape
    groups, hidden = lax.axis_size(expert), lax.axis_size("hidden")
    slots = slot_params.shape[1]
    wide = weight_in.shape[1]
    rows = images * count
    weight_in, weight_out = weight_in[0], weight_out[0]
    by_token = jnp.transpose(tokens, (1, 0, 2))
    grad_by_token = jnp.transpose(cotangent, (1, 0, 2))
    table = pltpu.VMEM((slots, rows), f32)
    row_shape = pltpu.VMEM((rows, width), bf16)
    held_shape = pltpu.VMEM(by_token.shape, bf16)
    sent_shape = pltpu.VMEM((groups, hidden, images, 2 * width), bf16)

    part, token_rows, keys = call(
        lambda *refs: logits_kernel(lax.axis_size("expert_c"), *refs),
        [table, row_shape, pltpu.VMEM((slots, width), bf16)],
        (),
        "logits",
        far=(by_token, jnp.transpose(slot_params)),
        scratch=[held_shape, pltpu.VMEM((slots, width), bf16), pltpu.SemaphoreType.DMA((2,))],
    )
    grad_rows, *expert_values = call(
        lambda *refs: prepare_kernel("hidden", *refs),
        [
            row_shape,
            pltpu.VMEM((1, wide), f32),
            *[pltpu.VMEM(value.shape, bf16) for value in (bias_in, weight_out, weight_in)],
            *[pltpu.VMEM(value.shape[::-1], bf16) for value in (weight_out, weight_in)],
        ],
        (part,),
        "prepare",
        far=(grad_by_token, bias_out, bias_in, weight_out, weight_in),
        scratch=[
            held_shape,
            pltpu.VMEM(bias_out.shape, bf16),
            pltpu.SemaphoreType.DMA((3 + 2 * weight_pieces,)),
        ],
    )
    parts = exchange(part, "hidden", True)
    sent, dispatch, combine, total = call(
        lambda *refs: dispatch_kernel(images, hidden, *refs),
        [sent_shape, table, table, pltpu.VMEM((1, rows), f32)],
        (*parts, token_rows, grad_rows),
        "dispatch",
    )

    def to_all(value):
        value = value.reshape(groups * hidden, images, 2 * width)
        value = lax.all_to_all(value, send_order, split_axis=0, concat_axis=0, tiled=True)
        return value.reshape(groups, hidden, images, 2 * width)

    (sent,) = call(
        expert_kernel,
        [sent_shape],
        (to_all(sent), *expert_values),
        "expert",
        24,
    )
    slot_out, in_grad, part = call(
        gradient_kernel,
        [*[pltpu.VMEM((slots * images, width), bf16)] * 2, pltpu.VMEM((slots, rows), bf16)],
        (to_all(sent), token_rows, grad_rows, dispatch, combine),
        "gradient",
    )
    parts = exchange(part, "hidden", False)
    mixed, direct, zloss = call(
        mixed_kernel,
        [held_shape, pltpu.VMEM((rows, width), f32), pltpu.VMEM((images, count), f32)],
        (dispatch, combine, total, slot_out, in_grad),
        "mixed",
    )
    out_shape = jax.ShapeDtypeStruct(by_token.shape, bf16)
    token_grad, mixed, zloss = call(
        lambda *refs: token_kernel(hidden, *refs),
        [out_shape, out_shape, jax.ShapeDtypeStruct((images, count), f32)],
        (*parts, combine, total, keys, direct, mixed, zloss),
        "token_grad",
        far_outs=True,
        scratch=[held_shape, pltpu.SemaphoreType.DMA((3,))],
    )
    return (jnp.transpose(mixed, (1, 0, 2)), jnp.transpose(token_grad, (1, 0, 2)), zloss)


def solution(mesh):
    groups, hidden = mesh.devices.shape
    halves = 2 if groups % 4 == 0 else 1
    parts = (halves, groups // (halves * halves), halves, hidden)
    return jax.shard_map(
        per_device,
        mesh=jax.sharding.Mesh(mesh.devices.reshape(parts), (*expert, "hidden")),
        in_specs=(
            P(expert, None, "hidden"),
            P("hidden", None),
            P(expert, None, "hidden"),
            P(expert, "hidden"),
            P(expert, "hidden", None),
            P(expert, "hidden"),
            P(expert, None, "hidden"),
        ),
        out_specs=(P(expert, None, "hidden"), P(expert, None, "hidden"), P(expert, None)),
        check_vma=False,
    )
```
